256 devices in a mesh: row: 8 (over x, z_hi), col: 32 (over y, z_lo, core).
Axes of the slice: x: 4, y: 4, z: 8 (z_hi: 2, z_lo: 4; z = z_hi * 4 + z_lo), core: 2. Of those that a mesh axis runs over, the one named last changes fastest.
Arguments:
- inputs: bfloat16 [1024, 12288], P('col', 'row'), may hold values from -6 to 6
- preact: bfloat16 [1024, 24576], P('row', 'col'), may hold values from -6 to 6
- w_in: bfloat16 [12288, 24576], P('row', 'col'), may hold values from -0.0546875 to 0.0546875
- w_out: bfloat16 [24576, 12288], P('col', 'row'), may hold values from -0.0390625 to 0.0390625
- out_grad: bfloat16 [1024, 12288], P('col', 'row'), may hold values from -27 to 27
Outputs:
- input_grad: bfloat16 [1024, 12288], P('col', 'row')
- w_in_grad: bfloat16 [12288, 24576], P('row', 'col')
- w_out_grad: bfloat16 [24576, 12288], P('col', 'row')
- amaxes: float32 [2], replicated
The draws below stay inside these ranges and needn't reach their ends.
All inputs are finite; a program needn't handle non-finite values. Where the reference program divides by a largest or mean magnitude, that divisor is 1e-20 or more.
Results may differ from the reference program's by a relative error of at most 0.0058.
Values may be sent and summed in bfloat16 or wider, within the bound.
No kernel may reach another device: no remote copies, remote signals or barrier semaphores. Data moves between devices by JAX's collectives and lax.ppermute only.
A program may use at most 64 MiB of HBM per device.

```python
import math
import jax
import jax.numpy as jnp

D = 12288
FF = 24576
TOKENS = 1024


def draw_out_grad(key, part):
    key = jax.random.fold_in(key, 7)
    base = jnp.clip(jax.random.normal(key, (TOKENS, D), jnp.float32), -3.0, 3.0)
    tok_scale = 1.0 + 2.0 * jnp.arange(TOKENS, dtype=jnp.float32) / (TOKENS - 1)
    feat_scale = 1.0 + 2.0 * jnp.arange(D, dtype=jnp.float32) / (D - 1)
    return (base * tok_scale[:, None] * feat_scale[None, :]).astype(jnp.bfloat16)


def shard_levels(stream_key, shape, split, smallest, high):
    loudness = 1.0
    for axis_at, blocks in split:
        draws = jax.random.uniform(jax.random.fold_in(jax.random.fold_in(stream_key, 6), axis_at), (blocks,), jnp.float32, smallest / len(split), high / len(split))
        loudness = loudness * jnp.repeat(jnp.exp(draws), shape[axis_at] // blocks).reshape((-1,) + (1,) * (len(shape) - 1 - axis_at))
    return loudness


def noise(own_key, dims, scale, bound, shards=(), held_as=jnp.bfloat16):
    level = shard_levels(own_key, dims, shards, -0.22, 0.18) if shards else 1.0
    values = jax.random.normal(own_key, dims, jnp.float32) * scale * level
    return jnp.minimum(jnp.maximum(values, -bound), bound).astype(held_as)


def setup_inputs(seed: int = 0) -> dict:
    keys = jax.random.split(jax.random.key(seed), 6)
    inputs = noise(keys[0], (TOKENS, D), 1.0, 6.0, ((0, 32), (1, 8)))
    preact = noise(keys[1], (TOKENS, FF), 1.0, 6.0, ((0, 8), (1, 32)))
    w_in = noise(keys[2], (D, FF), D ** -0.5, 0.0546875, ((0, 8), (1, 32)))
    w_out = noise(keys[3], (FF, D), FF ** -0.5, 0.0390625, ((0, 32), (1, 8)))
    out_grad = draw_out_grad(jax.random.fold_in(keys[5], 71), 0)
    return dict(inputs=inputs, preact=preact, w_in=w_in, w_out=w_out, out_grad=out_grad)


coef = math.sqrt(2.0 / math.pi)

def gelu_parts(pre):
    inner = coef * (pre + 0.044715 * pre * pre * pre)
    tval = jnp.tanh(inner)
    value = 0.5 * pre * (1.0 + tval)
    slope = 0.5 * (1.0 + tval) + 0.5 * pre * (1.0 - tval * tval) * coef * (1.0 + 3.0 * 0.044715 * pre * pre)
    return (value, slope)

def reference(inputs, preact, w_in, w_out, out_grad):
    amax_y = jnp.max(jnp.abs(out_grad.astype(jnp.float32)))
    s_y = 448.0 / (amax_y + 1e-06)
    grad_q = (out_grad.astype(jnp.float32) * s_y).astype(jnp.bfloat16)
    back = jnp.dot(grad_q, w_out.T, preferred_element_type=jnp.float32)
    value, slope = gelu_parts(preact.astype(jnp.float32))
    hidden_grad = back / s_y * slope
    amax_h = jnp.max(jnp.abs(hidden_grad))
    s_h = 448.0 / (amax_h + 1e-06)
    hidden_q = (hidden_grad * s_h).astype(jnp.bfloat16)
    hidden = value.astype(jnp.bfloat16)
    w_out_grad = (jnp.dot(hidden.T, grad_q, preferred_element_type=jnp.float32) / s_y).astype(jnp.bfloat16)
    w_in_grad = (jnp.dot(inputs.T, hidden_q, preferred_element_type=jnp.float32) / s_h).astype(jnp.bfloat16)
    input_grad = (jnp.dot(hidden_q, w_in.T, preferred_element_type=jnp.float32) / s_h).astype(jnp.bfloat16)
    amaxes = jnp.stack([amax_y, amax_h])
    return (input_grad, w_in_grad, w_out_grad, amaxes)
```

```python
import math

import jax
import jax.numpy as jnp
from jax import lax
from jax.sharding import PartitionSpec as P

coef = math.sqrt(2.0 / math.pi)
f32, bf16 = jnp.float32, jnp.bfloat16
CHUNKS = 1


def gelu_parts(pre):
    inner = coef * (pre + 0.044715 * pre * pre * pre)
    tval = jnp.tanh(inner)
    value = 0.5 * pre * (1.0 + tval)
    slope = 0.5 * (1.0 + tval) + 0.5 * pre * (1.0 - tval * tval) * coef * (
        1.0 + 3.0 * 0.044715 * pre * pre
    )
    return (value, slope)


def dot(left, right, dims):
    return lax.dot_general(left, right, (dims, ((), ())), preferred_element_type=f32)


def to_core(v):
    return lax.ppermute(v, "col", [(i, i ^ 1) for i in range(32)])


def to_l(v, k):
    return lax.ppermute(v, "col", [(i, i ^ (2 * k)) for i in range(32)])


def to_y(v, k):
    return lax.ppermute(v, "col", [(i, (i + 8 * k) % 32) for i in range(32)])


def to_x(v, k):
    return lax.ppermute(v, "row", [(i, (i + 2 * k) % 8) for i in range(8)])


def to_h(v):
    return lax.ppermute(v, "row", [(i, i ^ 1) for i in range(8)])


def pick(stacked, at):
    return lax.dynamic_index_in_dim(stacked, at, 0, keepdims=False)


def place(blocks, spots):
    out = jnp.zeros((len(blocks),) + blocks[0].shape, blocks[0].dtype)
    for block, spot in zip(blocks, spots):
        out = lax.dynamic_update_index_in_dim(out, block, spot, 0)
    return out


def by_core(c, mine, other, axis):
    first = jnp.where(c == 0, mine, other)
    second = jnp.where(c == 0, other, mine)
    return jnp.stack([first, second], axis=axis)


def spread_max(v):
    for axis, size, bits in (("row", 8, (1, 2, 4)), ("col", 32, (1, 2, 4, 8, 16))):
        for bit in bits:
            v = jnp.maximum(v, lax.ppermute(v, axis, [(i, i ^ bit) for i in range(size)]))
    return v


def local(inputs, preact, w_in, w_out, out_grad):
    row, col = lax.axis_index("row"), lax.axis_index("col")
    x, h = row // 2, row % 2
    y, l, c = col // 8, (col // 2) % 4, col % 2
    n = 32 // CHUNKS
    d, ff = out_grad.shape[1], preact.shape[1]

    inputs_all = lax.all_gather(inputs, "col", axis=0, tiled=True)
    value, _ = gelu_parts(preact.astype(f32))
    hidden_all = lax.all_gather(value.astype(bf16), "row", axis=0, tiled=True)

    w_out_both = jnp.concatenate([w_out, to_core(w_out)], axis=0)
    w_in_both = jnp.concatenate([w_in, to_core(w_in)], axis=1)
    pre = preact.reshape(4, 32, ff)
    pre_mine = jnp.stack([pick(pre, c), pick(pre, 2 + c)])
    pre_other = jnp.stack([pick(pre, 1 - c), pick(pre, 3 - c)])
    pre_mine = jnp.concatenate([pre_mine, to_core(pre_other)], axis=-1)
    pre_two = by_core(h, pre_mine, to_h(pre_mine), 0).reshape(4, 32, 2 * ff)
    pre_two = lax.optimization_barrier(pre_two)
    _, slope = gelu_parts(pre_two.astype(f32))

    grads, hqs, outs = [], [], []
    top = jnp.zeros((), f32)
    for s in range(CHUNKS):
        rows = slice(s * n, (s + 1) * n)
        mine = out_grad[rows]
        got = place([mine] + [to_l(mine, k) for k in (1, 2, 3)], [l, l ^ 1, l ^ 2, l ^ 3])
        got = got.reshape(4 * n, d)
        grad = place([got] + [to_y(got, k) for k in (1, 2, 3)], [(y - k) % 4 for k in range(4)])
        grads.append(grad.reshape(4, 4, n, d))

        back = None
        parts = []
        for j in (2, 1, 3):
            part = dot(pick(grad, (x + j) % 4), w_out_both, ((1,), (1,))).astype(bf16)
            parts.append(to_x(part, j))
        back = dot(pick(grad, x), w_out_both, ((1,), (1,)))
        for part in parts:
            back = back + part.astype(f32)
        sent = back.astype(bf16)
        back = sent.astype(f32) + to_h(sent).astype(f32)
        hidden_grad = back.reshape(4, n, 2 * ff) * slope[:, rows]
        top = jnp.maximum(top, jnp.max(jnp.abs(hidden_grad)))
        hq = hidden_grad.astype(bf16).reshape(4 * n, 2 * ff)
        hq_all = place([hq] + [to_x(hq, k) for k in (1, 2, 3)], [(x - k) % 4 for k in range(4)])
        hqs.append(hq_all.reshape(4, 4, n, 2 * ff))

        parts = []
        for k in (2, 1, 3):
            part = dot(pick(hq_all, (y + k) % 4), w_in_both, ((1,), (1,))).astype(bf16)
            parts.append(to_y(part, k))
        total = dot(pick(hq_all, y), w_in_both, ((1,), (1,)))
        for part in parts:
            total = total + part.astype(f32)
        total = total.reshape(4, n, d)
        out = pick(total, l)
        for k in (1, 2, 3):
            out = out + to_l(pick(total, l ^ k).astype(bf16), k).astype(f32)
        outs.append(out.astype(bf16))
    input_grad = jnp.concatenate(outs, axis=0)

    grad = jnp.concatenate(grads, axis=2)
    grad_all = lax.optimization_barrier(by_core(c, grad, to_core(grad), 2).reshape(1024, d))
    w_out_grad = dot(hidden_all, grad_all, ((0,), (0,))).astype(bf16)
    hq = jnp.concatenate(hqs, axis=2)
    hq_all = lax.optimization_barrier(by_core(c, hq[..., :ff], to_core(hq[..., ff:]), 2).reshape(1024, ff))
    w_in_grad = dot(inputs_all, hq_all, ((0,), (0,))).astype(bf16)

    amax_y = jnp.max(jnp.abs(out_grad.astype(f32)))
    both = jnp.where(lax.broadcasted_iota(jnp.int32, (8, 128), 0) == 0, amax_y, top)
    amaxes = spread_max(both)[:2, 0]
    return (input_grad, w_in_grad, w_out_grad, amaxes)


def solution(mesh):
    placed = (P("col", "row"), P("row", "col"), P("row", "col"), P("col", "row"), P("col", "row"))
    return jax.shard_map(
        local,
        mesh=mesh,
        in_specs=placed,
        out_specs=(P("col", "row"), P("row", "col"), P("col", "row"), P()),
        check_vma=False,
    )
```

```python
import math

import jax
import jax.numpy as jnp
from jax import lax
from jax.sharding import PartitionSpec as P

coef = math.sqrt(2.0 / math.pi)
f32, bf16 = jnp.float32, jnp.bfloat16
barrier = lax.optimization_barrier


def gelu_value(pre):
    inner = coef * (pre + 0.044715 * pre * pre * pre)
    return 0.5 * pre * (1.0 + jnp.tanh(inner))


def gelu_slope(pre):
    inner = coef * (pre + 0.044715 * pre * pre * pre)
    tval = jnp.tanh(inner)
    return 0.5 * (1.0 + tval) + 0.5 * pre * (1.0 - tval * tval) * coef * (
        1.0 + 3.0 * 0.044715 * pre * pre
    )


def dot(left, right, dims):
    return lax.dot_general(left, right, (dims, ((), ())), preferred_element_type=f32)


def across(left, right):
    return dot(left, right, ((1,), (1,)))


def over_tokens(left, right):
    return dot(left, right, ((0,), (0,)))


def to_core(v):
    return lax.ppermute(v, "col", [(i, i ^ 1) for i in range(32)])


def to_l(v, k):
    return lax.ppermute(v, "col", [(i, i ^ (2 * k)) for i in range(32)])


def to_y(v, k):
    return lax.ppermute(v, "col", [(i, (i + 8 * k) % 32) for i in range(32)])


def to_x(v, k):
    return lax.ppermute(v, "row", [(i, (i + 2 * k) % 8) for i in range(8)])


def to_h(v):
    return lax.ppermute(v, "row", [(i, i ^ 1) for i in range(8)])


def pick(stacked, at):
    return lax.dynamic_index_in_dim(stacked, at % stacked.shape[0], 0, keepdims=False)


def ring(v, send):
    far, near, behind = send(v, 2), send(v, 3), send(v, 1)
    return jnp.stack([v, near, far, behind])


def roll(v, by):
    return lax.dynamic_slice_in_dim(jnp.concatenate([v, v[:3]]), by % 4, 4, 0)


def flip(v, l, axis):
    shape = v.shape
    v = v.reshape(shape[:axis] + (2, 2) + shape[axis + 1 :])
    v = jnp.where(l % 2 == 1, jnp.flip(v, axis + 1), v)
    v = jnp.where(l >= 2, jnp.flip(v, axis), v)
    return v.reshape(shape)


def in_order(first, mine, other, axis):
    return jnp.stack([jnp.where(first, mine, other), jnp.where(first, other, mine)], axis=axis)


def spread_max(v):
    for axis, size, bits in (("row", 8, (2, 4, 1)), ("col", 32, (1, 2, 4, 8, 16))):
        for bit in bits:
            v = jnp.maximum(v, lax.ppermute(v, axis, [(i, i ^ bit) for i in range(size)]))
    return v


def local(inputs, preact, w_in, w_out, out_grad):
    row, col = lax.axis_index("row"), lax.axis_index("col")
    x, h = row // 2, row % 2
    y, l, c = col // 8, (col // 2) % 4, col % 2
    d, ff = out_grad.shape[1], preact.shape[1]

    grad = jnp.stack([out_grad] + [to_l(out_grad, k) for k in (1, 2, 3)]).reshape(128, d)
    w_out_o = to_core(w_out)
    grad = ring(grad, to_y)

    pre = barrier(in_order(h == 0, preact, to_h(preact), 0).reshape(4, 2, 32, ff))
    pre = jnp.stack([pick(pre, l ^ m) for m in range(4)])
    pre = jnp.stack([jnp.where(c == 0, pre[:, 0], pre[:, 1]), jnp.where(c == 0, pre[:, 1], pre[:, 0])])
    pre = barrier(pre.reshape(2, 128, ff))
    pre_a, pre_b = pre[0], to_core(pre[1])
    slopes = [gelu_slope(barrier(p).astype(f32)) for p in (pre_a, pre_b)]
    pre_all = barrier(roll(ring(pre, to_x), y - x).reshape(1024, ff))
    hidden_all = gelu_value(pre_all.astype(f32)).astype(bf16)
    w_in_o = to_core(w_in)
    inputs, _ = barrier((inputs, grad))
    inputs_all = lax.all_gather(inputs, "col", axis=0, tiled=True)

    top = jnp.zeros((), f32)
    hqs = []
    for slope, weight in zip(slopes, (w_out, w_out_o)):
        parts = [to_x(across(pick(grad, x - y + j), weight).astype(bf16), j) for j in (2, 1, 3)]
        back = across(pick(grad, x - y), weight)
        for part in parts:
            back = back + part.astype(f32)
        sent = back.astype(bf16)
        hidden_grad = (sent.astype(f32) + to_h(sent).astype(f32)) * slope
        top = jnp.maximum(top, jnp.max(jnp.abs(hidden_grad)))
        hqs.append(ring(hidden_grad.astype(bf16), to_x))
    hq_a, hq_b = hqs

    parts = []
    for k in (2, 1, 3, 0):
        at = y - x + k
        part = across(pick(hq_a, at), w_in) + across(pick(hq_b, at), w_in_o)
        parts.append(part if k == 0 else to_y(part.astype(bf16), k))
    total = parts[3]
    for part in parts[:3]:
        total = total + part.astype(f32)
    total = total.reshape(4, 32, d)
    moved = [to_l(total[k].astype(bf16), k) for k in (3, 2, 1)]
    out = total[0]
    for part in moved:
        out = out + part.astype(f32)
    input_grad = out.astype(bf16)

    grad_all = jnp.stack([grad, to_core(grad)], axis=1).reshape(1024, d)
    w_out_grad = over_tokens(hidden_all, barrier(grad_all)).astype(bf16)
    mine, other = hq_a.reshape(4, 4, 32, ff), to_core(hq_b).reshape(4, 4, 32, ff)
    hq = flip(in_order(c == 0, mine, other, 2), l, 1)
    hq = barrier(roll(barrier(hq), -x).reshape(1024, ff))
    w_in_grad = over_tokens(inputs_all, hq).astype(bf16)

    amax_y = jnp.max(jnp.abs(out_grad.astype(f32)))
    top, _ = barrier((top, hq_b))
    both = jnp.where(lax.broadcasted_iota(jnp.int32, (8, 128), 0) == 0, amax_y, top)
    amaxes = spread_max(both)[:2, 0]
    return (input_grad, w_in_grad, w_out_grad, amaxes)


def solution(mesh):
    placed = (P("col", "row"), P("row", "col"), P("row", "col"), P("col", "row"), P("col", "row"))
    return jax.shard_map(
        local,
        mesh=mesh,
        in_specs=placed,
        out_specs=(P("col", "row"), P("row", "col"), P("col", "row"), P()),
        check_vma=False,
    )
```

```python
import math

import jax
import jax.numpy as jnp
from jax import lax
from jax.sharding import PartitionSpec as P

coef = math.sqrt(2.0 / math.pi)
f32, bf16 = jnp.float32, jnp.bfloat16
barrier = lax.optimization_barrier


def gelu_value(pre):
    inner = coef * (pre + 0.044715 * pre * pre * pre)
    return 0.5 * pre * (1.0 + jnp.tanh(inner))


def gelu_slope(pre):
    inner = coef * (pre + 0.044715 * pre * pre * pre)
    tval = jnp.tanh(inner)
    return 0.5 * (1.0 + tval) + 0.5 * pre * (1.0 - tval * tval) * coef * (
        1.0 + 3.0 * 0.044715 * pre * pre
    )


def dot(left, right, dims):
    return lax.dot_general(left, right, (dims, ((), ())), preferred_element_type=f32)


def across(left, right):
    return dot(left, right, ((1,), (1,)))


def over_tokens(left, right):
    return dot(left, right, ((0,), (0,)))


def to_core(v):
    return lax.ppermute(v, "col", [(i, i ^ 1) for i in range(32)])


def to_l(v, k):
    return lax.ppermute(v, "col", [(i, i ^ (2 * k)) for i in range(32)])


def to_y(v, k):
    return lax.ppermute(v, "col", [(i, (i + 8 * k) % 32) for i in range(32)])


def to_x(v, k):
    return lax.ppermute(v, "row", [(i, (i + 2 * k) % 8) for i in range(8)])


def to_h(v):
    return lax.ppermute(v, "row", [(i, i ^ 1) for i in range(8)])


def pick(stacked, at):
    return lax.dynamic_index_in_dim(stacked, at % stacked.shape[0], 0, keepdims=False)


def ring(v, send):
    far, near, behind = send(v, 2), send(v, 3), send(v, 1)
    return jnp.stack([v, near, far, behind])


def roll(v, by):
    return lax.dynamic_slice_in_dim(jnp.concatenate([v, v[:3]]), by % 4, 4, 0)


def flip(v, l, axis):
    shape = v.shape
    v = v.reshape(shape[:axis] + (2, 2) + shape[axis + 1 :])
    v = jnp.where(l % 2 == 1, jnp.flip(v, axis + 1), v)
    v = jnp.where(l >= 2, jnp.flip(v, axis), v)
    return v.reshape(shape)


def in_order(first, mine, other, axis):
    return jnp.stack([jnp.where(first, mine, other), jnp.where(first, other, mine)], axis=axis)


def lanes(v):
    return jnp.max(jnp.abs(v.astype(f32)).reshape(-1, 128), axis=0)


def rounded(v):
    return lax.reduce_precision(v, 8, 7)


def pack(v, top_h, top_y):
    high = rounded(top_h)
    mid = rounded(top_h - high)
    low = top_h - high - mid
    extra = jnp.stack([high, mid, low, top_y]).astype(bf16)
    extra = jnp.pad(extra, ((0, v.shape[0] - 4), (0, 0)))
    return jnp.concatenate([v.astype(bf16), extra], axis=1)


def unpack(v):
    extra = v[:4, -128:].astype(f32)
    return v[:, :-128], extra[0] + extra[1] + extra[2], extra[3]


def local(inputs, preact, w_in, w_out, out_grad):
    row, col = lax.axis_index("row"), lax.axis_index("col")
    x, h = row // 2, row % 2
    y, l, c = col // 8, (col // 2) % 4, col % 2
    d, ff = out_grad.shape[1], preact.shape[1]

    grad = jnp.stack([out_grad] + [to_l(out_grad, k) for k in (1, 2, 3)]).reshape(128, d)
    w_out_both = jnp.concatenate([w_out, to_core(w_out)], axis=0)
    grad = ring(grad, to_y)

    pre = barrier(in_order(h == 0, preact, to_h(preact), 0).reshape(4, 2, 32, ff))
    pre = jnp.stack([pick(pre, l ^ m) for m in range(4)])
    pre = jnp.stack([jnp.where(c == 0, pre[:, 0], pre[:, 1]), jnp.where(c == 0, pre[:, 1], pre[:, 0])])
    pre = barrier(pre.reshape(2, 128, ff))
    pre_mine = barrier(jnp.concatenate([pre[0], to_core(pre[1])], axis=1))
    slope = gelu_slope(pre_mine.astype(f32))
    pre_all = barrier(roll(ring(pre, to_x), y - x).reshape(1024, ff))
    hidden_all = gelu_value(pre_all.astype(f32)).astype(bf16)
    w_in_both = jnp.concatenate([w_in, to_core(w_in)], axis=1)
    inputs, grad = barrier((inputs, grad))
    inputs_all = lax.all_gather(inputs, "col", axis=0, tiled=True)
    top_y = lanes(grad)

    parts = [to_x(across(pick(grad, x - y + j), w_out_both).astype(bf16), j) for j in (2, 1, 3)]
    back = across(pick(grad, x - y), w_out_both)
    for part in parts:
        back = back + part.astype(f32)
    back = rounded(back)
    none = jnp.zeros((128,), f32)
    other, _, other_y = unpack(to_h(pack(back, none, top_y)))
    top_y = jnp.maximum(top_y, other_y)
    hidden_grad = (back + other.astype(f32)) * slope
    top_h = lanes(hidden_grad)
    hq = ring(pack(hidden_grad, top_h, top_y), to_x)
    for j in range(1, 4):
        _, far_h, far_y = unpack(hq[j])
        top_h, top_y = jnp.maximum(top_h, far_h), jnp.maximum(top_y, far_y)

    grad_all = jnp.stack([grad, to_core(grad)], axis=1).reshape(1024, d)
    w_out_grad = over_tokens(hidden_all, barrier(grad_all)).astype(bf16)
    hq, w_out_grad = barrier((hq, w_out_grad))

    parts = []
    for k in (2, 1, 3, 0):
        part = across(pick(hq, y - x + k)[:, : 2 * ff], w_in_both)
        parts.append(part if k == 0 else to_y(pack(part, top_h, top_y), k))

    mine = hq[:, :, :ff].reshape(4, 4, 32, ff)
    theirs = to_core(hq[:, :, ff : 2 * ff]).reshape(4, 4, 32, ff)
    hq = flip(in_order(c == 0, mine, theirs, 2), l, 1)
    hq = barrier(roll(barrier(hq), -x).reshape(1024, ff))
    w_in_grad = over_tokens(inputs_all, hq).astype(bf16)

    total = parts[3]
    for part in parts[:3]:
        part, far_h, far_y = unpack(part)
        total = total + part.astype(f32)
        top_h, top_y = jnp.maximum(top_h, far_h), jnp.maximum(top_y, far_y)
    total, w_in_grad = barrier((total, w_in_grad))
    total = total.reshape(4, 32, d)
    moved = [to_l(pack(total[k], top_h, top_y), k) for k in (3, 2, 1)]
    out = total[0]
    for part in moved:
        part, far_h, far_y = unpack(part)
        out = out + part.astype(f32)
        top_h, top_y = jnp.maximum(top_h, far_h), jnp.maximum(top_y, far_y)
    input_grad = out.astype(bf16)

    tops = jnp.stack([top_y, top_h] + [none] * 6)
    amaxes = jnp.max(jnp.maximum(tops, to_core(tops)), axis=1)[:2]
    return (input_grad, w_in_grad, w_out_grad, amaxes)


def solution(mesh):
    placed = (P("col", "row"), P("row", "col"), P("row", "col"), P("col", "row"), P("col", "row"))
    return jax.shard_map(
        local,
        mesh=mesh,
        in_specs=placed,
        out_specs=(P("col", "row"), P("row", "col"), P("col", "row"), P()),
        check_vma=False,
    )
```

```python
import math

import jax
import jax.numpy as jnp
from jax import lax
from jax.experimental import pallas as pl
from jax.experimental.pallas import tpu as pltpu
from jax.sharding import PartitionSpec as P

coef = math.sqrt(2.0 / math.pi)
f32, bf16 = jnp.float32, jnp.bfloat16
barrier = lax.optimization_barrier
D, FF, T = 1536, 768, 128
W = 2 * FF
B = 256


def gelu_value(pre):
    inner = coef * (pre + 0.044715 * pre * pre * pre)
    return 0.5 * pre * (1.0 + jnp.tanh(inner))


def gelu_slope(pre):
    inner = coef * (pre + 0.044715 * pre * pre * pre)
    tval = jnp.tanh(inner)
    return 0.5 * (1.0 + tval) + 0.5 * pre * (1.0 - tval * tval) * coef * (
        1.0 + 3.0 * 0.044715 * pre * pre
    )


def across(left, right):
    return lax.dot_general(left, right, (((1,), (1,)), ((), ())), preferred_element_type=f32)


def over_tokens(left, right):
    return lax.dot_general(left, right, (((0,), (0,)), ((), ())), preferred_element_type=f32)


def to_core(v):
    return lax.ppermute(v, "col", [(i, i ^ 1) for i in range(32)])


def to_l(v, k):
    return lax.ppermute(v, "col", [(i, i ^ (2 * k)) for i in range(32)])


def to_y(v, k):
    return lax.ppermute(v, "col", [(i, (i + 8 * k) % 32) for i in range(32)])


def to_x(v, k):
    return lax.ppermute(v, "row", [(i, (i + 2 * k) % 8) for i in range(8)])


def to_h(v):
    return lax.ppermute(v, "row", [(i, i ^ 1) for i in range(8)])


def pick(stacked, at):
    return lax.dynamic_index_in_dim(stacked, at % stacked.shape[0], 0, keepdims=False)


def ring(v, send):
    far, near, behind = send(v, 2), send(v, 3), send(v, 1)
    return [v, near, far, behind]


def put_tops(ref, top_h, top_y):
    row = lax.broadcasted_iota(jnp.int32, (ref.shape[0], 128), 0)
    high = top_h.astype(bf16).astype(f32)
    mid = (top_h - high).astype(bf16).astype(f32)
    low = top_h - high - mid
    extra = jnp.where(row == 0, high, jnp.where(row == 1, mid, jnp.where(row == 2, low, 0.0)))
    ref[:, D : D + 128] = jnp.where(row == 3, top_y, extra).astype(bf16)


def get_tops(refs):
    top_h = top_y = jnp.zeros((1, 128), f32)
    for ref in refs:
        extra = ref[0:16, D : D + 128].astype(f32)
        top_h = jnp.maximum(top_h, extra[0:1] + extra[1:2] + extra[2:3])
        top_y = jnp.maximum(top_y, extra[3:4])
    return top_h, top_y


def spots(shift, s):
    return (s - shift + 4) & 3


def back_kernel(t, g0, g1, g2, g3, wa, wb, own, p1, p2, p3, stacked, blocks):
    i = pl.program_id(0)

    @pl.when(i == 0)
    def _():
        for s, g in enumerate((g0, g1, g2, g3)):
            blocks[spots(t[0], s)] = g[...]
            stacked[s * T : (s + 1) * T] = g[...]

    def work(w):
        out = across(blocks[...].reshape(4 * T, D), w[...])
        at = pl.ds(pl.multiple_of(i * B, B), B)
        own[:, at] = out[:T]
        for k, p in enumerate((p1, p2, p3)):
            p[:, at] = out[(k + 1) * T : (k + 2) * T].astype(bf16)

    pl.when(i < FF // B)(lambda: work(wa))
    pl.when(i >= FF // B)(lambda: work(wb))


def sum_kernel(own, r1, r2, r3, tops, msg):
    for k in range(T // 16):
        at = slice(16 * k, 16 * (k + 1))
        total = own[at] + r1[at].astype(f32) + r2[at].astype(f32) + r3[at].astype(f32)
        msg[at, :W] = total.astype(bf16)
    put_tops(msg, jnp.zeros((1, 128), f32), tops[0:1])


def slope_kernel(mine, other, pre, msg):
    _, top_y = get_tops((mine, other))
    top = jnp.zeros((16, W), f32)
    for k in range(T // 16):
        at = slice(16 * k, 16 * (k + 1))
        back = mine[at, :W].astype(f32) + other[at, :W].astype(f32)
        hidden_grad = back * gelu_slope(pre[at].astype(f32))
        top = jnp.maximum(top, jnp.abs(hidden_grad))
        msg[at, :W] = hidden_grad.astype(bf16)
    top = jnp.max(top, axis=0, keepdims=True)
    top_h = top[:, :128]
    for k in range(1, W // 128):
        top_h = jnp.maximum(top_h, top[:, 128 * k : 128 * (k + 1)])
    put_tops(msg, top_h, top_y)


def grad_kernel(t, m0, m1, m2, m3, wa, wb, own, p1, p2, p3, qa, qb, blocks):
    i = pl.program_id(0)

    @pl.when(i == 0)
    def _():
        for s, m in enumerate((m0, m1, m2, m3)):
            blocks[spots(t[0], s)] = m[:, :W]
            qa[s * T : (s + 1) * T] = m[:, :FF]
            qb[s * T : (s + 1) * T] = m[:, FF:W]
        top_h, top_y = get_tops((m0, m1, m2, m3))
        for p in (p1, p2, p3):
            put_tops(p, top_h, top_y)

    hq = blocks[...].reshape(4 * T, W)
    out = across(hq[:, :FF], wa[...]) + across(hq[:, FF:], wb[...])
    at = pl.ds(pl.multiple_of(i * B, B), B)
    own[:, at] = out[:T]
    for k, p in enumerate((p1, p2, p3)):
        p[:, at] = out[(k + 1) * T : (k + 2) * T].astype(bf16)


def gather_kernel(own, r1, r2, r3, mine, kept, s1, s2, s3):
    top_h, top_y = get_tops((r1, r2, r3, mine))
    for m, out in enumerate((kept, s1, s2, s3)):
        at = slice(32 * m, 32 * (m + 1))
        total = own[at] + r1[at, :D].astype(f32) + r2[at, :D].astype(f32) + r3[at, :D].astype(f32)
        out[:, :D] = total.astype(out.dtype)
    for out in (s1, s2, s3):
        put_tops(out, top_h, top_y)


def last_kernel(kept, r1, r2, r3, mine, out, tops):
    top_h, top_y = get_tops((r1, r2, r3, mine))
    total = kept[...] + r1[:, :D].astype(f32) + r2[:, :D].astype(f32) + r3[:, :D].astype(f32)
    out[...] = total.astype(bf16)
    row = lax.broadcasted_iota(jnp.int32, (8, 128), 0)
    tops[...] = jnp.where(row == 0, top_y, jnp.where(row == 1, top_h, 0.0))


def w_out_kernel(t, r0, r1, r2, r3, mine, other, out, hidden):
    @pl.when(pl.program_id(0) == 0)
    def _():
        for s, r in enumerate((r0, r1, r2, r3)):
            k = spots(t[0], s)
            for c in range(2):
                hidden[c, k] = gelu_value(r[c].astype(f32)).astype(bf16)

    half = hidden[...].reshape(2, 4 * T, FF)
    out[...] = (over_tokens(half[0], mine[...]) + over_tokens(half[1], other[...])).astype(bf16)


def w_in_kernel(at, inputs, mine, other, out, hq):
    @pl.when(pl.program_id(0) == 0)
    def _():
        x, l, c = at[0], at[1], at[2]
        for k in range(4):
            for m in range(4):
                rows = slice(k * T + m * 32, k * T + (m + 1) * 32)
                to = ((x + k) & 3) * 4 + (l ^ m)
                hq[to, c] = mine[rows]
                hq[to, 1 - c] = other[rows]

    out[...] = over_tokens(inputs[...], hq[...].reshape(8 * T, FF)).astype(bf16)


def like(*shape, dtype=bf16):
    return jax.ShapeDtypeStruct(shape, dtype)


def call(kernel, name, outs, args, flops=0, **spec):
    outs = list(outs)
    size = sum(math.prod(a.shape) * a.dtype.itemsize for a in list(args) + outs)
    return pl.pallas_call(
        kernel,
        out_shape=outs,
        name=name,
        compiler_params=pltpu.CompilerParams(vmem_limit_bytes=30 * 2**20),
        cost_estimate=pl.CostEstimate(flops=flops, bytes_accessed=size, transcendentals=0),
        **spec,
    )(*args)


def whole(a):
    zeros = (0,) * len(a.shape)
    return pl.BlockSpec(a.shape, lambda i, t: zeros)


def local(inputs, preact, w_in, w_out, out_grad):
    row, col = lax.axis_index("row"), lax.axis_index("col")
    x, h = row // 2, row % 2
    y, l, c = col // 8, (col // 2) % 4, col % 2
    steps = D // B
    big = 2 * 4 * T * D * W

    grad = jnp.stack([out_grad] + [to_l(out_grad, k) for k in (1, 2, 3)]).reshape(T, D)
    w_out_o = to_core(w_out)
    top_y = jnp.broadcast_to(jnp.max(jnp.abs(out_grad)).astype(f32), (8, 128))
    grad, preact, w_in_late = barrier((grad, preact, w_in))
    grads = ring(grad, to_y)

    pre = preact.reshape(2, 2, 32, FF)
    theirs = to_h(preact).reshape(2, 2, 32, FF)
    pre = jnp.stack([jnp.where(h == 0, pre, theirs), jnp.where(h == 0, theirs, pre)])
    pre = barrier(pre.reshape(4, 2, 32, FF))
    pre = jnp.stack([pick(pre, l ^ m) for m in range(4)])
    pre = jnp.stack([jnp.where(c == 0, pre[:, 0], pre[:, 1]), jnp.where(c == 0, pre[:, 1], pre[:, 0])])
    pre = barrier(pre.reshape(2, T, FF))
    pre_mine = barrier(jnp.concatenate([pre[0], to_core(pre[1])], axis=1))
    w_in_o = to_core(w_in_late)

    *grads, inputs = barrier((*grads, inputs))
    inputs_all = lax.all_gather(inputs, "col", axis=0, tiled=True)

    args = (jnp.reshape((x - y) & 3, (1,)).astype(jnp.int32), *grads, w_out, w_out_o)
    outs = [like(T, W, dtype=f32)] + [like(T, W)] * 3 + [like(4 * T, D)]
    last = FF // B - 1
    own, p1, p2, p3, stacked = call(
        back_kernel,
        "back",
        outs,
        args,
        big,
        grid_spec=pltpu.PrefetchScalarGridSpec(
            num_scalar_prefetch=1,
            grid=(W // B,),
            in_specs=[whole(g) for g in grads]
            + [
                pl.BlockSpec((B, D), lambda i, t: (jnp.minimum(i, last), 0)),
                pl.BlockSpec((B, D), lambda i, t: (jnp.maximum(i - last - 1, 0), 0)),
            ],
            out_specs=[whole(o) for o in outs],
            scratch_shapes=[pltpu.VMEM((4, T, D), bf16)],
        ),
    )
    r2, r1, r3 = to_x(p2, 2), to_x(p1, 1), to_x(p3, 3)
    (sent,) = call(sum_kernel, "back_sum", [like(T, W + 128)], (own, r1, r2, r3, top_y))
    other = to_h(sent)
    pre, sent = barrier((pre, sent))
    pres = ring(pre, to_x)
    stacked_o = to_core(stacked)
    (msg,) = call(slope_kernel, "slope", [like(T, W + 128)], (sent, other, pre_mine))
    msgs = ring(msg, to_x)

    turn = jnp.reshape((y - x) & 3, (1,)).astype(jnp.int32)
    args = (turn, *pres, stacked, stacked_o)
    outs = [like(FF, D)]
    (w_out_grad,) = call(
        w_out_kernel,
        "w_out_grad",
        outs,
        args,
        big,
        grid_spec=pltpu.PrefetchScalarGridSpec(
            num_scalar_prefetch=1,
            grid=(steps,),
            in_specs=[whole(p) for p in pres] + [pl.BlockSpec((4 * T, B), lambda i, t: (0, i))] * 2,
            out_specs=[pl.BlockSpec((FF, B), lambda i, t: (0, i))],
            scratch_shapes=[pltpu.VMEM((2, 4, T, FF), bf16)],
        ),
    )
    *far, w_out_grad = barrier((*msgs[1:], w_out_grad))
    msgs = [msgs[0], *far]

    args = (turn, *msgs, w_in, w_in_o)
    outs = [like(T, D, dtype=f32)] + [like(T, D + 128)] * 3 + [like(4 * T, FF)] * 2
    own, p1, p2, p3, hq_a, hq_b = call(
        grad_kernel,
        "input_grad",
        outs,
        args,
        big,
        grid_spec=pltpu.PrefetchScalarGridSpec(
            num_scalar_prefetch=1,
            grid=(steps,),
            in_specs=[whole(m) for m in msgs] + [pl.BlockSpec((B, FF), lambda i, t: (i, 0))] * 2,
            out_specs=[whole(o) for o in outs],
            scratch_shapes=[pltpu.VMEM((4, T, W), bf16)],
        ),
    )
    r2, r1, r3 = to_y(p2, 2), to_y(p1, 1), to_y(p3, 3)
    hq_b = to_core(hq_b)
    outs = [like(D, FF)]
    (w_in_grad,) = call(
        w_in_kernel,
        "w_in_grad",
        outs,
        (jnp.stack([x, l, c]).astype(jnp.int32), inputs_all, hq_a, hq_b),
        big,
        grid_spec=pltpu.PrefetchScalarGridSpec(
            num_scalar_prefetch=1,
            grid=(steps,),
            in_specs=[pl.BlockSpec((8 * T, B), lambda i, t: (0, i)), whole(hq_a), whole(hq_b)],
            out_specs=[pl.BlockSpec((B, FF), lambda i, t: (i, 0))],
            scratch_shapes=[pltpu.VMEM((16, 2, 32, FF), bf16)],
        ),
    )
    r1, r2, r3, w_in_grad = barrier((r1, r2, r3, w_in_grad))
    outs = [like(32, D, dtype=f32)] + [like(32, D + 128)] * 3
    kept, s1, s2, s3 = call(gather_kernel, "y_sum", outs, (own, r1, r2, r3, p1))
    r2, r3, r1 = to_l(s2, 2), to_l(s3, 3), to_l(s1, 1)
    outs = [like(32, D), like(8, 128, dtype=f32)]
    input_grad, tops = call(last_kernel, "l_sum", outs, (kept, r1, r2, r3, s1))
    amaxes = jnp.max(jnp.maximum(tops, to_core(tops)), axis=1)[:2]
    return (input_grad, w_in_grad, w_out_grad, amaxes)


def solution(mesh):
    placed = (P("col", "row"), P("row", "col"), P("row", "col"), P("col", "row"), P("col", "row"))
    return jax.shard_map(
        local,
        mesh=mesh,
        in_specs=placed,
        out_specs=(P("col", "row"), P("row", "col"), P("col", "row"), P()),
        check_vma=False,
    )
```

```python
import math

import jax
import jax.numpy as jnp
from jax import lax
from jax.experimental import pallas as pl
from jax.experimental.pallas import tpu as pltpu
from jax.sharding import PartitionSpec as P

coef = math.sqrt(2.0 / math.pi)
f32, bf16 = jnp.float32, jnp.bfloat16
barrier = lax.optimization_barrier
D, FF, T = 1536, 768, 128
W = 2 * FF
B = 256


def gelu_value(pre):
    inner = coef * (pre + 0.044715 * pre * pre * pre)
    return 0.5 * pre * (1.0 + jnp.tanh(inner))


def gelu_slope(pre):
    inner = coef * (pre + 0.044715 * pre * pre * pre)
    tval = jnp.tanh(inner)
    return 0.5 * (1.0 + tval) + 0.5 * pre * (1.0 - tval * tval) * coef * (
        1.0 + 3.0 * 0.044715 * pre * pre
    )


def across(left, right):
    return lax.dot_general(left, right, (((1,), (1,)), ((), ())), preferred_element_type=f32)


def over_tokens(left, right):
    return lax.dot_general(left, right, (((0,), (0,)), ((), ())), preferred_element_type=f32)


def to_core(v):
    return lax.ppermute(v, "col", [(i, i ^ 1) for i in range(32)])


def to_l(v, k):
    return lax.ppermute(v, "col", [(i, i ^ (2 * k)) for i in range(32)])


def to_y(v, k):
    return lax.ppermute(v, "col", [(i, (i + 8 * k) % 32) for i in range(32)])


def to_x(v, k):
    return lax.ppermute(v, "row", [(i, (i + 2 * k) % 8) for i in range(8)])


def to_h(v):
    return lax.ppermute(v, "row", [(i, i ^ 1) for i in range(8)])


def ring(v, send):
    far, near, behind = send(v, 2), send(v, 3), send(v, 1)
    return [v, near, far, behind]


def put_tops(ref, top_h, top_y):
    row = lax.broadcasted_iota(jnp.int32, (ref.shape[0], 128), 0)
    high = top_h.astype(bf16).astype(f32)
    mid = (top_h - high).astype(bf16).astype(f32)
    low = top_h - high - mid
    extra = jnp.where(row == 0, high, jnp.where(row == 1, mid, jnp.where(row == 2, low, 0.0)))
    ref[:, D : D + 128] = jnp.where(row == 3, top_y, extra).astype(bf16)


def get_tops(refs):
    top_h = top_y = jnp.zeros((1, 128), f32)
    for ref in refs:
        extra = ref[0:16, D : D + 128].astype(f32)
        top_h = jnp.maximum(top_h, extra[0:1] + extra[1:2] + extra[2:3])
        top_y = jnp.maximum(top_y, extra[3:4])
    return top_h, top_y


def place(at):
    row, col = at[0], at[1]
    return row >> 1, row & 1, col >> 3, (col >> 1) & 3, col & 1


def copy(src, dst, sem):
    return pltpu.make_async_copy(src, dst, sem)


def back_kernel(
    t, g0, g1, g2, g3, wa, wb, here, there, own, p1, p2, p3, stacked, pre, pre_other, blocks, weights, sems, wsems
):
    i = pl.program_id(0)
    x, h, y, l, c = place(t)
    shift = x - y
    last = FF // B

    def weight(k):
        ref, at = (wa, k) if k < last else (wb, k - last)
        return copy(ref.at[at * B : (at + 1) * B], weights.at[k], wsems.at[k])

    def moves():
        out = []
        for high in range(2):
            for low in range(2):
                for core in range(2):
                    rows = slice((low * 2 + core) * 32, (low * 2 + core + 1) * 32)
                    ref, slot = (here, there)[high], (2 * (h ^ high) + low) ^ l
                    out.append(copy(ref.at[rows], pre.at[c ^ core, slot], sems.at[5 + len(out)]))
        return out

    def blocks_in():
        return [copy(g, blocks.at[(s - shift) & 3], sems.at[s]) for s, g in enumerate((g0, g1, g2, g3))]

    @pl.when(i == 0)
    def _():
        for move in blocks_in():
            move.start()
        for k in range(W // B):
            weight(k).start()
        for move in moves():
            move.start()
        for move in blocks_in():
            move.wait()
        copy(blocks, stacked, sems.at[4]).start()

    for k in range(W // B):
        pl.when(i == k)(weight(k).wait)
    out = across(blocks[...].reshape(4 * T, D), weights[i])
    at = pl.ds(pl.multiple_of(i * B, B), B)
    own[:, at] = out[:T]
    for k, p in enumerate((p1, p2, p3)):
        p[:, at] = out[(k + 1) * T : (k + 2) * T].astype(bf16)

    @pl.when(i == 0)
    def _():
        for move in moves():
            move.wait()
        copy(pre.at[1], pre_other, sems.at[5]).start()

    @pl.when(i == pl.num_programs(0) - 1)
    def _():
        copy(pre.at[1], pre_other, sems.at[5]).wait()
        copy(blocks, stacked, sems.at[4]).wait()


def sum_kernel(own, r1, r2, r3, tops, msg):
    for k in range(T // 16):
        at = slice(16 * k, 16 * (k + 1))
        total = own[at] + r1[at].astype(f32) + r2[at].astype(f32) + r3[at].astype(f32)
        msg[at, :W] = total.astype(bf16)
    put_tops(msg, jnp.zeros((1, 128), f32), tops[0:1])


def slope_kernel(mine, other, pre_a, pre_b, msg):
    _, top_y = get_tops((mine, other))
    top = jnp.zeros((16, FF), f32)
    for k in range(T // 16):
        at = slice(16 * k, 16 * (k + 1))
        for half, pre in enumerate((pre_a, pre_b)):
            cols = slice(half * FF, (half + 1) * FF)
            back = mine[at, cols].astype(f32) + other[at, cols].astype(f32)
            hidden_grad = back * gelu_slope(pre[at].astype(f32))
            top = jnp.maximum(top, jnp.abs(hidden_grad))
            msg[at, cols] = hidden_grad.astype(bf16)
    top = jnp.max(top, axis=0, keepdims=True)
    top_h = top[:, :128]
    for k in range(1, FF // 128):
        top_h = jnp.maximum(top_h, top[:, 128 * k : 128 * (k + 1)])
    put_tops(msg, top_h, top_y)


def grad_kernel(t, m0, m1, m2, m3, wa, wb, own, p1, p2, p3, hq_b, blocks, weights, sems, wsems):
    i = pl.program_id(0)
    x, _, y, _, _ = place(t)

    def weight(k):
        rows = slice(k * B, (k + 1) * B)
        return [copy(w.at[rows], weights.at[s, k], wsems.at[s, k]) for s, w in enumerate((wa, wb))]

    def blocks_in():
        return [copy(m, blocks.at[(s - y + x) & 3], sems.at[s]) for s, m in enumerate((m0, m1, m2, m3))]

    def blocks_out():
        return [
            copy(blocks.at[(s - y + x) & 3, :, FF:W], hq_b.at[s * T : (s + 1) * T], sems.at[4 + s])
            for s in range(4)
        ]

    @pl.when(i == 0)
    def _():
        for move in blocks_in():
            move.start()
        for k in range(D // B):
            for move in weight(k):
                move.start()
        for move in blocks_in():
            move.wait()
        for move in blocks_out():
            move.start()
        top_h, top_y = get_tops([blocks.at[s] for s in range(4)])
        for p in (p1, p2, p3):
            put_tops(p, top_h, top_y)

    for k in range(D // B):

        @pl.when(i == k)
        def _():
            for move in weight(k):
                move.wait()

    hq = blocks[:, :, :W].reshape(4 * T, W)
    out = across(hq[:, :FF], weights[0, i]) + across(hq[:, FF:], weights[1, i])
    at = pl.ds(pl.multiple_of(i * B, B), B)
    own[:, at] = out[:T]
    for k, p in enumerate((p1, p2, p3)):
        p[:, at] = out[(k + 1) * T : (k + 2) * T].astype(bf16)

    @pl.when(i == pl.num_programs(0) - 1)
    def _():
        for move in blocks_out():
            move.wait()


def gather_kernel(own, r1, r2, r3, mine, kept, s1, s2, s3):
    top_h, top_y = get_tops((r1, r2, r3, mine))
    for m, out in enumerate((kept, s1, s2, s3)):
        at = slice(32 * m, 32 * (m + 1))
        total = own[at] + r1[at, :D].astype(f32) + r2[at, :D].astype(f32) + r3[at, :D].astype(f32)
        out[:, :D] = total.astype(out.dtype)
    for out in (s1, s2, s3):
        put_tops(out, top_h, top_y)


def last_kernel(kept, r1, r2, r3, mine, out, tops):
    top_h, top_y = get_tops((r1, r2, r3, mine))
    total = kept[...] + r1[:, :D].astype(f32) + r2[:, :D].astype(f32) + r3[:, :D].astype(f32)
    out[...] = total.astype(bf16)
    row = lax.broadcasted_iota(jnp.int32, (8, 128), 0)
    tops[...] = jnp.where(row == 0, top_y, jnp.where(row == 1, top_h, 0.0))


def w_out_kernel(r0, r1, r2, r3, mine, other, out, raw, hidden, grads, sems, gsems):
    i = pl.program_id(0)

    def parts(k):
        cols = slice(k * B, (k + 1) * B)
        return [copy(g.at[:, cols], grads.at[k, s], gsems.at[s, k]) for s, g in enumerate((mine, other))]

    def pres():
        return [copy(r, raw.at[s], sems.at[s]) for s, r in enumerate((r0, r1, r2, r3))]

    @pl.when(i == 0)
    def _():
        for move in pres():
            move.start()
        for k in range(D // B):
            for move in parts(k):
                move.start()
        for s, move in enumerate(pres()):
            move.wait()
            for c in range(2):
                hidden[c, s * T : (s + 1) * T] = gelu_value(raw[s, c].astype(f32)).astype(bf16)

    for k in range(D // B):

        @pl.when(i == k)
        def _():
            for move in parts(k):
                move.wait()

    half = grads[i]
    out[...] = (over_tokens(hidden[0], half[0]) + over_tokens(hidden[1], half[1])).astype(bf16)


def w_in_kernel(at, inputs, m0, m1, m2, m3, other, out, hq, cols, sems, csems):
    i = pl.program_id(0)
    x, _, _, l, c = place(at)

    def part(k):
        return copy(inputs.at[:, k * B : (k + 1) * B], cols.at[k], csems.at[k])

    def blocks_in():
        out = []
        for k, m in enumerate((m0, m1, m2, m3)):
            for s in range(4):
                to = ((x + k) & 3) * 4 + (s ^ l)
                rows = slice(s * 32, (s + 1) * 32)
                out.append(copy(m.at[rows, 0:FF], hq.at[to, c], sems.at[len(out)]))
                rows = slice(k * T + s * 32, k * T + (s + 1) * 32)
                out.append(copy(other.at[rows], hq.at[to, 1 - c], sems.at[len(out)]))
        return out

    @pl.when(i == 0)
    def _():
        for move in blocks_in():
            move.start()
        for k in range(D // B):
            part(k).start()
        for move in blocks_in():
            move.wait()

    for k in range(D // B):
        pl.when(i == k)(part(k).wait)
    out[...] = over_tokens(cols[i], hq[...].reshape(8 * T, FF)).astype(bf16)


def like(*shape, dtype=bf16):
    return jax.ShapeDtypeStruct(shape, dtype)


def call(kernel, name, outs, args, flops=0, mib=8, **spec):
    outs = list(outs)
    size = sum(math.prod(a.shape) * a.dtype.itemsize for a in list(args) + outs)
    return pl.pallas_call(
        kernel,
        out_shape=outs,
        name=name,
        compiler_params=pltpu.CompilerParams(vmem_limit_bytes=mib * 2**20),
        cost_estimate=pl.CostEstimate(flops=flops, bytes_accessed=size, transcendentals=0),
        **spec,
    )(*args)


def whole(a):
    zeros = (0,) * len(a.shape)
    return pl.BlockSpec(a.shape, lambda i, *t: zeros, pipeline_mode=pl.Buffered(1))


def here(args):
    return [pl.BlockSpec(memory_space=pltpu.HBM)] * len(args)


dma = pltpu.SemaphoreType.DMA


def local(inputs, preact, w_in, w_out, out_grad):
    row, col = lax.axis_index("row"), lax.axis_index("col")
    at, out_grad, inputs = barrier((jnp.stack([row, col]).astype(jnp.int32), out_grad, inputs))
    steps = D // B
    big = 2 * 4 * T * D * W

    inputs_all = lax.all_gather(inputs, "col", axis=0, tiled=True)

    grad = jnp.stack([out_grad] + [to_l(out_grad, k) for k in (1, 2, 3)]).reshape(T, D)
    w_out_o = to_core(w_out)
    top_y = jnp.broadcast_to(jnp.max(jnp.abs(out_grad)).astype(f32), (8, 128))
    grad, w_out_o, top_y, w_in_late, pre_late = barrier((grad, w_out_o, top_y, w_in, preact))
    grads = ring(grad, to_y)
    w_in_o = to_core(w_in_late)
    there = to_h(pre_late)
    *grads, w_in_o, there = barrier((*grads, w_in_o, there))

    args = (at, *grads, w_out, w_out_o, preact, there)
    outs = [like(T, W, dtype=f32)] + [like(T, W)] * 3
    apart = [like(4, T, D), like(2, 4, 32, FF), like(4, 32, FF)]
    own, p1, p2, p3, stacked, pre, pre_other = call(
        back_kernel,
        "back",
        outs + apart,
        args,
        big,
        20,
        grid_spec=pltpu.PrefetchScalarGridSpec(
            num_scalar_prefetch=1,
            grid=(W // B,),
            in_specs=here(args[1:]),
            out_specs=[whole(o) for o in outs] + here(apart),
            scratch_shapes=[
                pltpu.VMEM((4, T, D), bf16),
                pltpu.VMEM((W // B, B, D), bf16),
                dma((13,)),
                dma((W // B,)),
            ],
        ),
    )
    r2, r1, r3 = to_x(p2, 2), to_x(p1, 1), to_x(p3, 3)
    pre_b = to_core(pre_other.reshape(T, FF))
    r1, r2, r3, pre_b = barrier((r1, r2, r3, pre_b))

    (sent,) = call(sum_kernel, "back_sum", [like(T, W + 128)], (own, r1, r2, r3, top_y))
    other = to_h(sent)
    pre, sent = barrier((pre.reshape(2, T, FF), sent))
    pre_near, pre_behind = to_x(pre, 3), to_x(pre, 1)
    other, pre_near, pre_behind = barrier((other, pre_near, pre_behind))
    pre_a = pre[0]
    (msg,) = call(slope_kernel, "slope", [like(T, W + 128)], (sent, other, pre_a, pre_b))
    msgs = ring(msg, to_x)
    stacked, _ = barrier((stacked.reshape(4 * T, D), msg))
    stacked_o = to_core(stacked)
    *far, stacked_o = barrier((*msgs[1:], stacked_o))
    msgs = [msgs[0], *far]

    args = (at, *msgs, w_in, w_in_o)
    outs = [like(T, D, dtype=f32)] + [like(T, D + 128)] * 3
    apart = [like(4 * T, FF)]
    own, p1, p2, p3, hq_b = call(
        grad_kernel,
        "input_grad",
        outs + apart,
        args,
        big,
        20,
        grid_spec=pltpu.PrefetchScalarGridSpec(
            num_scalar_prefetch=1,
            grid=(steps,),
            in_specs=here(args[1:]),
            out_specs=[whole(o) for o in outs] + here(apart),
            scratch_shapes=[
                pltpu.VMEM((4, T, W + 128), bf16),
                pltpu.VMEM((2, steps, B, FF), bf16),
                dma((8,)),
                dma((2, steps)),
            ],
        ),
    )
    r2, r1, r3 = to_y(p2, 2), to_y(p1, 1), to_y(p3, 3)
    hq_o = to_core(hq_b)
    pre, _ = barrier((pre, hq_b))
    pre_far = to_x(pre, 2)
    args = (at, inputs_all, *msgs, hq_o)
    (w_in_grad,) = call(
        w_in_kernel,
        "w_in_grad",
        [like(D, FF)],
        args,
        big,
        20,
        grid_spec=pltpu.PrefetchScalarGridSpec(
            num_scalar_prefetch=1,
            grid=(steps,),
            in_specs=here(args[1:]),
            out_specs=[pl.BlockSpec((B, FF), lambda i, t: (i, 0))],
            scratch_shapes=[
                pltpu.VMEM((16, 2, 32, FF), bf16),
                pltpu.VMEM((steps, 8 * T, B), bf16),
                dma((32,)),
                dma((steps,)),
            ],
        ),
    )
    pre_far, w_in_grad = barrier((pre_far, w_in_grad))
    args = (pre, pre_near, pre_far, pre_behind, stacked, stacked_o)
    (w_out_grad,) = call(
        w_out_kernel,
        "w_out_grad",
        [like(FF, D)],
        args,
        big,
        20,
        grid=(steps,),
        in_specs=here(args),
        out_specs=[pl.BlockSpec((FF, B), lambda i: (0, i))],
        scratch_shapes=[
            pltpu.VMEM((4, 2, T, FF), bf16),
            pltpu.VMEM((2, 4 * T, FF), bf16),
            pltpu.VMEM((steps, 2, 4 * T, B), bf16),
            dma((4,)),
            dma((2, steps)),
        ],
    )
    r1, r2, r3, w_out_grad = barrier((r1, r2, r3, w_out_grad))
    outs = [like(32, D, dtype=f32)] + [like(32, D + 128)] * 3
    kept, s1, s2, s3 = call(gather_kernel, "y_sum", outs, (own, r1, r2, r3, p1))
    r2, r3, r1 = to_l(s2, 2), to_l(s3, 3), to_l(s1, 1)
    outs = [like(32, D), like(8, 128, dtype=f32)]
    input_grad, tops = call(last_kernel, "l_sum", outs, (kept, r1, r2, r3, s1))
    amaxes = jnp.max(jnp.maximum(tops, to_core(tops)), axis=1)[:2]
    return (input_grad, w_in_grad, w_out_grad, amaxes)


def solution(mesh):
    placed = (P("col", "row"), P("row", "col"), P("row", "col"), P("col", "row"), P("col", "row"))
    return jax.shard_map(
        local,
        mesh=mesh,
        in_specs=placed,
        out_specs=(P("col", "row"), P("row", "col"), P("col", "row"), P()),
        check_vma=False,
    )
```

```python
import math

import jax
import jax.numpy as jnp
from jax import lax
from jax.experimental import pallas as pl
from jax.experimental.pallas import tpu as pltpu
from jax.sharding import PartitionSpec as P

coef = math.sqrt(2.0 / math.pi)
f32, bf16 = jnp.float32, jnp.bfloat16
barrier = lax.optimization_barrier
D, FF, T = 1536, 768, 128
W = 2 * FF
B, C = 256, 768


def gelu_value(pre):
    inner = coef * (pre + 0.044715 * pre * pre * pre)
    return 0.5 * pre * (1.0 + jnp.tanh(inner))


def gelu_slope(pre):
    inner = coef * (pre + 0.044715 * pre * pre * pre)
    tval = jnp.tanh(inner)
    return 0.5 * (1.0 + tval) + 0.5 * pre * (1.0 - tval * tval) * coef * (
        1.0 + 3.0 * 0.044715 * pre * pre
    )


def across(left, right):
    return lax.dot_general(left, right, (((1,), (1,)), ((), ())), preferred_element_type=f32)


def over_tokens(left, right):
    return lax.dot_general(left, right, (((0,), (0,)), ((), ())), preferred_element_type=f32)


def to_core(v):
    return lax.ppermute(v, "col", [(i, i ^ 1) for i in range(32)])


def to_l(v, k):
    return lax.ppermute(v, "col", [(i, i ^ (2 * k)) for i in range(32)])


def to_y(v, k):
    return lax.ppermute(v, "col", [(i, (i + 8 * k) % 32) for i in range(32)])


def to_x(v, k):
    return lax.ppermute(v, "row", [(i, (i + 2 * k) % 8) for i in range(8)])


def to_h(v):
    return lax.ppermute(v, "row", [(i, i ^ 1) for i in range(8)])


def ring(v, send):
    far, near, behind = send(v, 2), send(v, 3), send(v, 1)
    return [v, near, far, behind]


def put_tops(ref, top_h, top_y):
    row = lax.broadcasted_iota(jnp.int32, (ref.shape[0], 128), 0)
    high = top_h.astype(bf16).astype(f32)
    mid = (top_h - high).astype(bf16).astype(f32)
    low = top_h - high - mid
    extra = jnp.where(row == 0, high, jnp.where(row == 1, mid, jnp.where(row == 2, low, 0.0)))
    ref[:, D : D + 128] = jnp.where(row == 3, top_y, extra).astype(bf16)


def get_tops(refs):
    top_h = top_y = jnp.zeros((1, 128), f32)
    for ref in refs:
        extra = ref[0:16, D : D + 128].astype(f32)
        top_h = jnp.maximum(top_h, extra[0:1] + extra[1:2] + extra[2:3])
        top_y = jnp.maximum(top_y, extra[3:4])
    return top_h, top_y


def stack_kernel(a0, a1, a2, a3, stacked, tops):
    for m, a in enumerate((a0, a1, a2, a3)):
        stacked[m * 32 : (m + 1) * 32] = a[...]
    top = jnp.max(jnp.abs(a0[...].astype(f32)), axis=0, keepdims=True)
    lanes = top[:, :128]
    for k in range(1, D // 128):
        lanes = jnp.maximum(lanes, top[:, 128 * k : 128 * (k + 1)])
    tops[...] = jnp.broadcast_to(lanes, (8, 128))


def place(at):
    row, col = at[0], at[1]
    return row >> 1, row & 1, col >> 3, (col >> 1) & 3, col & 1


def copy(src, dst, sem):
    return pltpu.make_async_copy(src, dst, sem)


def back_kernel(
    t, g0, g1, g2, g3, wa, wb, here, there, own, p1, p2, p3, stacked, pre, pre_other, blocks, weights, sems, wsems
):
    i = pl.program_id(0)
    x, h, y, l, c = place(t)
    shift = x - y
    last = FF // C

    def weight(k):
        ref, at = (wa, k) if k < last else (wb, k - last)
        return copy(ref.at[at * C : (at + 1) * C], weights.at[k], wsems.at[k])

    def moves():
        out = []
        for high in range(2):
            for low in range(2):
                for core in range(2):
                    rows = slice((low * 2 + core) * 32, (low * 2 + core + 1) * 32)
                    ref, slot = (here, there)[high], (2 * (h ^ high) + low) ^ l
                    out.append(copy(ref.at[rows], pre.at[c ^ core, slot], sems.at[5 + len(out)]))
        return out

    def blocks_in():
        return [copy(g, blocks.at[(s - shift) & 3], sems.at[s]) for s, g in enumerate((g0, g1, g2, g3))]

    @pl.when(i == 0)
    def _():
        for move in blocks_in():
            move.start()
        for k in range(W // C):
            weight(k).start()
        for move in moves():
            move.start()
        for move in blocks_in():
            move.wait()
        copy(blocks, stacked, sems.at[4]).start()

    for k in range(W // C):
        pl.when(i == k)(weight(k).wait)
    out = across(blocks[...].reshape(4 * T, D), weights[i])
    at = pl.ds(pl.multiple_of(i * C, C), C)
    own[:, at] = out[:T]
    for k, p in enumerate((p1, p2, p3)):
        p[:, at] = out[(k + 1) * T : (k + 2) * T].astype(bf16)

    @pl.when(i == 0)
    def _():
        for move in moves():
            move.wait()
        copy(pre.at[1], pre_other, sems.at[5]).start()

    @pl.when(i == pl.num_programs(0) - 1)
    def _():
        copy(pre.at[1], pre_other, sems.at[5]).wait()
        copy(blocks, stacked, sems.at[4]).wait()


def sum_kernel(own, r1, r2, r3, tops, msg):
    for k in range(T // 16):
        at = slice(16 * k, 16 * (k + 1))
        total = own[at] + r1[at].astype(f32) + r2[at].astype(f32) + r3[at].astype(f32)
        msg[at, :W] = total.astype(bf16)
    put_tops(msg, jnp.zeros((1, 128), f32), tops[0:1])


def slope_kernel(mine, other, pre_a, pre_b, msg):
    _, top_y = get_tops((mine, other))
    top = jnp.zeros((16, FF), f32)
    for k in range(T // 16):
        at = slice(16 * k, 16 * (k + 1))
        for half, pre in enumerate((pre_a, pre_b)):
            cols = slice(half * FF, (half + 1) * FF)
            back = mine[at, cols].astype(f32) + other[at, cols].astype(f32)
            hidden_grad = back * gelu_slope(pre[at].astype(f32))
            top = jnp.maximum(top, jnp.abs(hidden_grad))
            msg[at, cols] = hidden_grad.astype(bf16)
    top = jnp.max(top, axis=0, keepdims=True)
    top_h = top[:, :128]
    for k in range(1, FF // 128):
        top_h = jnp.maximum(top_h, top[:, 128 * k : 128 * (k + 1)])
    put_tops(msg, top_h, top_y)


def grad_kernel(t, m0, m1, m2, m3, wa, wb, own, p1, p2, p3, hq_b, blocks, weights, sems, wsems):
    i = pl.program_id(0)
    x, _, y, _, _ = place(t)

    def weight(k):
        rows = slice(k * C, (k + 1) * C)
        return [copy(w.at[rows], weights.at[s, k], wsems.at[s, k]) for s, w in enumerate((wa, wb))]

    def blocks_in():
        return [copy(m, blocks.at[(s - y + x) & 3], sems.at[s]) for s, m in enumerate((m0, m1, m2, m3))]

    def blocks_out():
        return [
            copy(blocks.at[(s - y + x) & 3, :, FF:W], hq_b.at[s * T : (s + 1) * T], sems.at[4 + s])
            for s in range(4)
        ]

    @pl.when(i == 0)
    def _():
        for move in blocks_in():
            move.start()
        for k in range(D // C):
            for move in weight(k):
                move.start()
        for move in blocks_in():
            move.wait()
        for move in blocks_out():
            move.start()
        top_h, top_y = get_tops([blocks.at[s] for s in range(4)])
        for p in (p1, p2, p3):
            put_tops(p, top_h, top_y)

    for k in range(D // C):

        @pl.when(i == k)
        def _():
            for move in weight(k):
                move.wait()

    hq = blocks[:, :, :W].reshape(4 * T, W)
    out = across(hq[:, :FF], weights[0, i]) + across(hq[:, FF:], weights[1, i])
    at = pl.ds(pl.multiple_of(i * C, C), C)
    own[:, at] = out[:T]
    for k, p in enumerate((p1, p2, p3)):
        p[:, at] = out[(k + 1) * T : (k + 2) * T].astype(bf16)

    @pl.when(i == pl.num_programs(0) - 1)
    def _():
        for move in blocks_out():
            move.wait()


def gather_kernel(own, r1, r2, r3, mine, kept, s1, s2, s3):
    top_h, top_y = get_tops((r1, r2, r3, mine))
    for m, out in enumerate((kept, s1, s2, s3)):
        at = slice(32 * m, 32 * (m + 1))
        total = own[at] + r1[at, :D].astype(f32) + r2[at, :D].astype(f32) + r3[at, :D].astype(f32)
        out[:, :D] = total.astype(out.dtype)
    for out in (s1, s2, s3):
        put_tops(out, top_h, top_y)


def last_kernel(kept, r1, r2, r3, mine, out, tops):
    top_h, top_y = get_tops((r1, r2, r3, mine))
    total = kept[...] + r1[:, :D].astype(f32) + r2[:, :D].astype(f32) + r3[:, :D].astype(f32)
    out[...] = total.astype(bf16)
    row = lax.broadcasted_iota(jnp.int32, (8, 128), 0)
    tops[...] = jnp.where(row == 0, top_y, jnp.where(row == 1, top_h, 0.0))


def w_out_kernel(r0, r1, r2, r3, mine, other, out, raw, hidden, grads, sems, gsems):
    i = pl.program_id(0)

    def parts(k):
        cols = slice(k * B, (k + 1) * B)
        return [copy(g.at[:, cols], grads.at[k, s], gsems.at[s, k]) for s, g in enumerate((mine, other))]

    def pres():
        return [copy(r, raw.at[s], sems.at[s]) for s, r in enumerate((r0, r1, r2, r3))]

    @pl.when(i == 0)
    def _():
        for move in pres():
            move.start()
        for k in range(D // B):
            for move in parts(k):
                move.start()
        for s, move in enumerate(pres()):
            move.wait()
            for c in range(2):
                hidden[c, s * T : (s + 1) * T] = gelu_value(raw[s, c].astype(f32)).astype(bf16)

    for k in range(D // B):

        @pl.when(i == k)
        def _():
            for move in parts(k):
                move.wait()

    half = grads[i]
    out[...] = (over_tokens(hidden[0], half[0]) + over_tokens(hidden[1], half[1])).astype(bf16)


def w_in_kernel(at, inputs, m0, m1, m2, m3, other, out, hq, cols, sems, csems):
    i = pl.program_id(0)
    x, _, _, l, c = place(at)

    def part(k):
        return copy(inputs.at[:, k * B : (k + 1) * B], cols.at[k], csems.at[k])

    def blocks_in():
        out = []
        for k, m in enumerate((m0, m1, m2, m3)):
            for s in range(4):
                to = ((x + k) & 3) * 4 + (s ^ l)
                rows = slice(s * 32, (s + 1) * 32)
                out.append(copy(m.at[rows, 0:FF], hq.at[to, c], sems.at[len(out)]))
                rows = slice(k * T + s * 32, k * T + (s + 1) * 32)
                out.append(copy(other.at[rows], hq.at[to, 1 - c], sems.at[len(out)]))
        return out

    @pl.when(i == 0)
    def _():
        for move in blocks_in():
            move.start()
        for k in range(D // B):
            part(k).start()
        for move in blocks_in():
            move.wait()

    for k in range(D // B):
        pl.when(i == k)(part(k).wait)
    out[...] = over_tokens(cols[i], hq[...].reshape(8 * T, FF)).astype(bf16)


def like(*shape, dtype=bf16):
    return jax.ShapeDtypeStruct(shape, dtype)


def call(kernel, name, outs, args, flops=0, mib=8, **spec):
    outs = list(outs)
    size = sum(math.prod(a.shape) * a.dtype.itemsize for a in list(args) + outs)
    return pl.pallas_call(
        kernel,
        out_shape=outs,
        name=name,
        compiler_params=pltpu.CompilerParams(vmem_limit_bytes=mib * 2**20),
        cost_estimate=pl.CostEstimate(flops=flops, bytes_accessed=size, transcendentals=0),
        **spec,
    )(*args)


def whole(a):
    zeros = (0,) * len(a.shape)
    return pl.BlockSpec(a.shape, lambda i, *t: zeros, pipeline_mode=pl.Buffered(1))


def here(args):
    return [pl.BlockSpec(memory_space=pltpu.HBM)] * len(args)


dma = pltpu.SemaphoreType.DMA


def local(inputs, preact, w_in, w_out, out_grad):
    row, col = lax.axis_index("row"), lax.axis_index("col")
    at, out_grad, inputs = barrier((jnp.stack([row, col]).astype(jnp.int32), out_grad, inputs))
    steps = D // B
    big = 2 * 4 * T * D * W

    inputs_all = lax.all_gather(inputs, "col", axis=0, tiled=True)

    got = [to_l(out_grad, k) for k in (1, 2, 3)]
    *got, w_out_late, pre_late = barrier((*got, w_out, preact))
    outs = [like(T, D), like(8, 128, dtype=f32)]
    grad, top_y = call(stack_kernel, "stack", outs, (out_grad, *got))
    grads = ring(grad, to_y)
    w_out_o = to_core(w_out_late)
    there = to_h(pre_late)
    *grads, w_out_o, there = barrier((*grads, w_out_o, there))

    args = (at, *grads, w_out, w_out_o, preact, there)
    outs = [like(T, W, dtype=f32)] + [like(T, W)] * 3
    apart = [like(4, T, D), like(2, 4, 32, FF), like(4, 32, FF)]
    own, p1, p2, p3, stacked, pre, pre_other = call(
        back_kernel,
        "back",
        outs + apart,
        args,
        big,
        20,
        grid_spec=pltpu.PrefetchScalarGridSpec(
            num_scalar_prefetch=1,
            grid=(W // C,),
            in_specs=here(args[1:]),
            out_specs=[whole(o) for o in outs] + here(apart),
            scratch_shapes=[
                pltpu.VMEM((4, T, D), bf16),
                pltpu.VMEM((W // C, C, D), bf16),
                dma((13,)),
                dma((W // C,)),
            ],
        ),
    )
    r2, r1, r3 = to_x(p2, 2), to_x(p1, 1), to_x(p3, 3)
    pre_b = to_core(pre_other.reshape(T, FF))
    r1, r2, r3, pre_b = barrier((r1, r2, r3, pre_b))

    (sent,) = call(sum_kernel, "back_sum", [like(T, W + 128)], (own, r1, r2, r3, top_y))
    other = to_h(sent)
    pre, sent, w_in_late = barrier((pre.reshape(2, T, FF), sent, w_in))
    w_in_o = to_core(w_in_late)
    pre_near, pre_behind, pre_far = to_x(pre, 3), to_x(pre, 1), to_x(pre, 2)
    other, pre_near, pre_behind, pre_far, w_in_o = barrier((other, pre_near, pre_behind, pre_far, w_in_o))
    pre_a = pre[0]
    (msg,) = call(slope_kernel, "slope", [like(T, W + 128)], (sent, other, pre_a, pre_b))
    msgs = ring(msg, to_x)
    stacked, _ = barrier((stacked.reshape(4 * T, D), msg))
    stacked_o = to_core(stacked)
    args = (pre, pre_near, pre_far, pre_behind, stacked, stacked_o)
    (w_out_grad,) = call(
        w_out_kernel,
        "w_out_grad",
        [like(FF, D)],
        args,
        big,
        20,
        grid=(steps,),
        in_specs=here(args),
        out_specs=[pl.BlockSpec((FF, B), lambda i: (0, i))],
        scratch_shapes=[
            pltpu.VMEM((4, 2, T, FF), bf16),
            pltpu.VMEM((2, 4 * T, FF), bf16),
            pltpu.VMEM((steps, 2, 4 * T, B), bf16),
            dma((4,)),
            dma((2, steps)),
        ],
    )
    *far, w_out_grad = barrier((*msgs[1:], w_out_grad))
    msgs = [msgs[0], *far]

    args = (at, *msgs, w_in, w_in_o)
    outs = [like(T, D, dtype=f32)] + [like(T, D + 128)] * 3
    apart = [like(4 * T, FF)]
    own, p1, p2, p3, hq_b = call(
        grad_kernel,
        "input_grad",
        outs + apart,
        args,
        big,
        20,
        grid_spec=pltpu.PrefetchScalarGridSpec(
            num_scalar_prefetch=1,
            grid=(D // C,),
            in_specs=here(args[1:]),
            out_specs=[whole(o) for o in outs] + here(apart),
            scratch_shapes=[
                pltpu.VMEM((4, T, W + 128), bf16),
                pltpu.VMEM((2, D // C, C, FF), bf16),
                dma((8,)),
                dma((2, D // C)),
            ],
        ),
    )
    r2, r1, r3 = to_y(p2, 2), to_y(p1, 1), to_y(p3, 3)
    hq_o = to_core(hq_b)
    args = (at, inputs_all, *msgs, hq_o)
    (w_in_grad,) = call(
        w_in_kernel,
        "w_in_grad",
        [like(D, FF)],
        args,
        big,
        20,
        grid_spec=pltpu.PrefetchScalarGridSpec(
            num_scalar_prefetch=1,
            grid=(steps,),
            in_specs=here(args[1:]),
            out_specs=[pl.BlockSpec((B, FF), lambda i, t: (i, 0))],
            scratch_shapes=[
                pltpu.VMEM((16, 2, 32, FF), bf16),
                pltpu.VMEM((steps, 8 * T, B), bf16),
                dma((32,)),
                dma((steps,)),
            ],
        ),
    )
    r1, r2, r3, w_in_grad = barrier((r1, r2, r3, w_in_grad))
    outs = [like(32, D, dtype=f32)] + [like(32, D + 128)] * 3
    kept, s1, s2, s3 = call(gather_kernel, "y_sum", outs, (own, r1, r2, r3, p1))
    r2, r3, r1 = to_l(s2, 2), to_l(s3, 3), to_l(s1, 1)
    outs = [like(32, D), like(8, 128, dtype=f32)]
    input_grad, tops = call(last_kernel, "l_sum", outs, (kept, r1, r2, r3, s1))
    amaxes = jnp.max(jnp.maximum(tops, to_core(tops)), axis=1)[:2]
    return (input_grad, w_in_grad, w_out_grad, amaxes)


def solution(mesh):
    placed = (P("col", "row"), P("row", "col"), P("row", "col"), P("col", "row"), P("col", "row"))
    return jax.shard_map(
        local,
        mesh=mesh,
        in_specs=placed,
        out_specs=(P("col", "row"), P("row", "col"), P("col", "row"), P()),
        check_vma=False,
    )
```

```python
import math

import jax
import jax.numpy as jnp
from jax import lax
from jax.experimental import pallas as pl
from jax.experimental.pallas import tpu as pltpu
from jax.sharding import PartitionSpec as P

coef = math.sqrt(2.0 / math.pi)
f32, bf16 = jnp.float32, jnp.bfloat16
barrier = lax.optimization_barrier
D, FF, T = 1536, 768, 128
W = 2 * FF
B, C = 256, 768


def gelu_value(pre):
    inner = coef * (pre + 0.044715 * pre * pre * pre)
    return 0.5 * pre * (1.0 + jnp.tanh(inner))


def gelu_slope(pre):
    inner = coef * (pre + 0.044715 * pre * pre * pre)
    tval = jnp.tanh(inner)
    return 0.5 * (1.0 + tval) + 0.5 * pre * (1.0 - tval * tval) * coef * (
        1.0 + 3.0 * 0.044715 * pre * pre
    )


def across(left, right):
    return lax.dot_general(left, right, (((1,), (1,)), ((), ())), preferred_element_type=f32)


def over_tokens(left, right):
    return lax.dot_general(left, right, (((0,), (0,)), ((), ())), preferred_element_type=f32)


def to_core(v):
    return lax.ppermute(v, "col", [(i, i ^ 1) for i in range(32)])


def to_l(v, k):
    return lax.ppermute(v, "col", [(i, i ^ (2 * k)) for i in range(32)])


def to_y(v, k):
    return lax.ppermute(v, "col", [(i, (i + 8 * k) % 32) for i in range(32)])


def to_x(v, k):
    return lax.ppermute(v, "row", [(i, (i + 2 * k) % 8) for i in range(8)])


def to_h(v):
    return lax.ppermute(v, "row", [(i, i ^ 1) for i in range(8)])


def ring(v, send):
    far, near, behind = send(v, 2), send(v, 3), send(v, 1)
    return [v, near, far, behind]


def message(rows):
    return like(W // 128 * rows + 16, 128)


def tile(c, rows, first=0, count=None):
    return slice(c * rows + first, c * rows + first + (count or rows))


def put_tops(ref, top_h, top_y):
    row = lax.broadcasted_iota(jnp.int32, (16, 128), 0)
    high = top_h.astype(bf16).astype(f32)
    mid = (top_h - high).astype(bf16).astype(f32)
    low = top_h - high - mid
    extra = jnp.where(row == 0, high, jnp.where(row == 1, mid, jnp.where(row == 2, low, 0.0)))
    ref[ref.shape[0] - 16 :] = jnp.where(row == 3, top_y, extra).astype(bf16)


def get_tops(refs):
    top_h = top_y = jnp.zeros((1, 128), f32)
    for ref in refs:
        extra = ref[ref.shape[0] - 16 :].astype(f32)
        top_h = jnp.maximum(top_h, extra[0:1] + extra[1:2] + extra[2:3])
        top_y = jnp.maximum(top_y, extra[3:4])
    return top_h, top_y


def columns(c):
    return slice(c * 128, (c + 1) * 128)


def stack_kernel(a0, a1, a2, a3, stacked, tops):
    for m, a in enumerate((a0, a1, a2, a3)):
        stacked[m * 32 : (m + 1) * 32] = a[...]
    top = jnp.max(jnp.abs(a0[...].astype(f32)), axis=0, keepdims=True)
    lanes = top[:, :128]
    for k in range(1, D // 128):
        lanes = jnp.maximum(lanes, top[:, 128 * k : 128 * (k + 1)])
    tops[...] = jnp.broadcast_to(lanes, (8, 128))


def join_kernel(a0, a1, a2, a3, out, sems):
    moves = [copy(a, out.at[k], sems.at[k]) for k, a in enumerate((a0, a1, a2, a3))]
    for move in moves:
        move.start()
    for move in moves:
        move.wait()


def place(at):
    row, col = at[0], at[1]
    return row >> 1, row & 1, col >> 3, (col >> 1) & 3, col & 1


def copy(src, dst, sem):
    return pltpu.make_async_copy(src, dst, sem)


def back_kernel(
    t, g0, g1, g2, g3, wa, wb, here, there, own, p1, p2, p3, stacked, pre, pre_other, blocks, weights, sems, wsems
):
    i = pl.program_id(0)
    x, h, y, l, c = place(t)
    shift = x - y
    last = FF // C

    def weight(k):
        ref, at = (wa, k) if k < last else (wb, k - last)
        return copy(ref.at[at * C : (at + 1) * C], weights.at[k], wsems.at[k])

    def moves():
        out = []
        for high in range(2):
            for low in range(2):
                for core in range(2):
                    rows = slice((low * 2 + core) * 32, (low * 2 + core + 1) * 32)
                    ref, slot = (here, there)[high], (2 * (h ^ high) + low) ^ l
                    out.append(copy(ref.at[rows], pre.at[c ^ core, slot], sems.at[5 + len(out)]))
        return out

    def blocks_in():
        return [copy(g, blocks.at[(s - shift) & 3], sems.at[s]) for s, g in enumerate((g0, g1, g2, g3))]

    @pl.when(i == 0)
    def _():
        for move in blocks_in():
            move.start()
        for k in range(W // C):
            weight(k).start()
        for move in moves():
            move.start()
        for move in blocks_in():
            move.wait()
        copy(blocks, stacked, sems.at[4]).start()

    for k in range(W // C):
        pl.when(i == k)(weight(k).wait)
    out = across(blocks[...].reshape(4 * T, D), weights[i])
    at = pl.ds(pl.multiple_of(i * C, C), C)
    own[:, at] = out[:T]
    for k, p in enumerate((p1, p2, p3)):
        p[:, at] = out[(k + 1) * T : (k + 2) * T].astype(bf16)

    @pl.when(i == 0)
    def _():
        for move in moves():
            move.wait()
        copy(pre.at[1], pre_other, sems.at[5]).start()

    @pl.when(i == pl.num_programs(0) - 1)
    def _():
        copy(pre.at[1], pre_other, sems.at[5]).wait()
        copy(blocks, stacked, sems.at[4]).wait()


def sum_kernel(own, r1, r2, r3, tops, msg):
    for c in range(W // 128):
        at = (slice(None), columns(c))
        total = own[at] + r1[at].astype(f32) + r2[at].astype(f32) + r3[at].astype(f32)
        msg[tile(c, T)] = total.astype(bf16)
    put_tops(msg, jnp.zeros((1, 128), f32), tops[0:1])


def slope_kernel(mine, other, pre_a, pre_b, msg):
    _, top_y = get_tops((mine, other))
    top_h = jnp.zeros((1, 128), f32)
    for c in range(W // 128):
        pre, k = (pre_a, c) if c < FF // 128 else (pre_b, c - FF // 128)
        back = mine[tile(c, T)].astype(f32) + other[tile(c, T)].astype(f32)
        hidden_grad = back * gelu_slope(pre[:, columns(k)].astype(f32))
        top_h = jnp.maximum(top_h, jnp.max(jnp.abs(hidden_grad), axis=0, keepdims=True))
        msg[tile(c, T)] = hidden_grad.astype(bf16)
    put_tops(msg, top_h, top_y)


def grad_kernel(t, m0, m1, m2, m3, wa, wb, own, p1, p2, p3, hq_a, hq_b, blocks, weights, sems, wsems):
    i = pl.program_id(0)
    x, _, y, _, _ = place(t)
    half = FF // 128

    def weight(k):
        rows = slice(k * C, (k + 1) * C)
        return [copy(w.at[rows], weights.at[s, k], wsems.at[s, k]) for s, w in enumerate((wa, wb))]

    def blocks_in():
        return [copy(m, blocks.at[(s - y + x) & 3], sems.at[s]) for s, m in enumerate((m0, m1, m2, m3))]

    def blocks_out():
        return [
            copy(
                blocks.at[(s - y + x) & 3, tile(k * half + c, T)],
                out.at[s * T : (s + 1) * T, columns(c)],
                sems.at[4 + (k * 4 + s) * half + c],
            )
            for k, out in enumerate((hq_a, hq_b))
            for s in range(4)
            for c in range(half)
        ]

    @pl.when(i == 0)
    def _():
        for move in blocks_in():
            move.start()
        for k in range(D // C):
            for move in weight(k):
                move.start()
        for move in blocks_in():
            move.wait()
        for move in blocks_out():
            move.start()
        top_h, top_y = get_tops([blocks.at[s] for s in range(4)])
        for p in (p1, p2, p3):
            put_tops(p, top_h, top_y)

    for k in range(D // C):

        @pl.when(i == k)
        def _():
            for move in weight(k):
                move.wait()

    tiles = [blocks[:, tile(c, T)].reshape(4 * T, 128) for c in range(2 * half)]
    hq = [jnp.concatenate(part, axis=1) for part in (tiles[:half], tiles[half:])]
    out = across(hq[0], weights[0, i]) + across(hq[1], weights[1, i])
    own[:, pl.ds(pl.multiple_of(i * C, C), C)] = out[:T]
    for k, p in enumerate((p1, p2, p3)):
        for c in range(C // 128):
            rows = pl.ds(pl.multiple_of((i * (C // 128) + c) * T, T), T)
            p[rows] = out[(k + 1) * T : (k + 2) * T, columns(c)].astype(bf16)

    @pl.when(i == pl.num_programs(0) - 1)
    def _():
        for move in blocks_out():
            move.wait()


def gather_kernel(own, r1, r2, r3, mine, kept, s1, s2, s3):
    top_h, top_y = get_tops((r1, r2, r3, mine))
    for m, out in enumerate((kept, s1, s2, s3)):
        for c in range(D // 128):
            at = tile(c, T, 32 * m, 32)
            total = own[32 * m : 32 * (m + 1), columns(c)]
            total = total + r1[at].astype(f32) + r2[at].astype(f32) + r3[at].astype(f32)
            if m:
                out[tile(c, 32)] = total.astype(bf16)
            else:
                out[:, columns(c)] = total
    for out in (s1, s2, s3):
        put_tops(out, top_h, top_y)


def last_kernel(kept, r1, r2, r3, mine, out, tops):
    top_h, top_y = get_tops((r1, r2, r3, mine))
    for c in range(D // 128):
        at = tile(c, 32)
        total = kept[:, columns(c)] + r1[at].astype(f32) + r2[at].astype(f32) + r3[at].astype(f32)
        out[:, columns(c)] = total.astype(bf16)
    row = lax.broadcasted_iota(jnp.int32, (8, 128), 0)
    tops[...] = jnp.where(row == 0, top_y, jnp.where(row == 1, top_h, 0.0))


def w_out_kernel(r0, r1, r2, r3, mine, other, out, raw, hidden, grads, sems, gsems):
    i = pl.program_id(0)

    def parts(k):
        cols = slice(k * B, (k + 1) * B)
        return [copy(g.at[:, cols], grads.at[k, s], gsems.at[s, k]) for s, g in enumerate((mine, other))]

    def pres():
        return [copy(r, raw.at[s], sems.at[s]) for s, r in enumerate((r0, r1, r2, r3))]

    @pl.when(i == 0)
    def _():
        for move in pres():
            move.start()
        for k in range(D // B):
            for move in parts(k):
                move.start()
        for s, move in enumerate(pres()):
            move.wait()
            for c in range(2):
                hidden[c, s * T : (s + 1) * T] = gelu_value(raw[s, c].astype(f32)).astype(bf16)

    for k in range(D // B):

        @pl.when(i == k)
        def _():
            for move in parts(k):
                move.wait()

    half = grads[i]
    out[...] = (over_tokens(hidden[0], half[0]) + over_tokens(hidden[1], half[1])).astype(bf16)


def w_in_kernel(t, inputs, inputs_o, mine, other, out, hq, cols, sems, csems):
    i = pl.program_id(0)
    x, _, y, _, _ = place(t)

    def parts(k):
        at = slice(k * B, (k + 1) * B)
        return [copy(a.at[:, :, at], cols.at[k, s], csems.at[s, k]) for s, a in enumerate((inputs, inputs_o))]

    def blocks_in():
        return [
            copy(ref.at[k * T : (k + 1) * T], hq.at[s, (k + x - y) & 3], sems.at[4 * s + k])
            for s, ref in enumerate((mine, other))
            for k in range(4)
        ]

    @pl.when(i == 0)
    def _():
        for move in blocks_in():
            move.start()
        for k in range(D // B):
            for move in parts(k):
                move.start()
        for move in blocks_in():
            move.wait()

    for k in range(D // B):

        @pl.when(i == k)
        def _():
            for move in parts(k):
                move.wait()

    out[...] = over_tokens(cols[i].reshape(8 * T, B), hq[...].reshape(8 * T, FF)).astype(bf16)


def like(*shape, dtype=bf16):
    return jax.ShapeDtypeStruct(shape, dtype)


def call(kernel, name, outs, args, flops=0, mib=8, **spec):
    outs = list(outs)
    size = sum(math.prod(a.shape) * a.dtype.itemsize for a in list(args) + outs)
    return pl.pallas_call(
        kernel,
        out_shape=outs,
        name=name,
        compiler_params=pltpu.CompilerParams(vmem_limit_bytes=mib * 2**20),
        cost_estimate=pl.CostEstimate(flops=flops, bytes_accessed=size, transcendentals=0),
        **spec,
    )(*args)


def whole(a):
    zeros = (0,) * len(a.shape)
    return pl.BlockSpec(a.shape, lambda i, *t: zeros, pipeline_mode=pl.Buffered(1))


def here(args):
    return [pl.BlockSpec(memory_space=pltpu.HBM)] * len(args)


dma = pltpu.SemaphoreType.DMA


def local(inputs, preact, w_in, w_out, out_grad):
    row, col = lax.axis_index("row"), lax.axis_index("col")
    at, out_grad, inputs = barrier((jnp.stack([row, col]).astype(jnp.int32), out_grad, inputs))
    steps = D // B
    big = 2 * 4 * T * D * W

    got = [to_l(out_grad, k) for k in (1, 2, 3)]
    w_out_o = to_core(w_out)
    *got, w_out_o, pre_late, w_in_late = barrier((*got, w_out_o, preact, w_in))
    outs = [like(T, D), like(8, 128, dtype=f32)]
    grad, top_y = call(stack_kernel, "stack", outs, (out_grad, *got))
    grads = ring(grad, to_y)
    w_in_o = to_core(w_in_late)
    there = to_h(pre_late)
    *grads, w_in_o, there = barrier((*grads, w_in_o, there))

    args = (at, *grads, w_out, w_out_o, preact, there)
    outs = [like(T, W, dtype=f32)] + [like(T, W)] * 3
    apart = [like(4, T, D), like(2, 4, 32, FF), like(4, 32, FF)]
    own, p1, p2, p3, stacked, pre, pre_other = call(
        back_kernel,
        "back",
        outs + apart,
        args,
        big,
        20,
        grid_spec=pltpu.PrefetchScalarGridSpec(
            num_scalar_prefetch=1,
            grid=(W // C,),
            in_specs=here(args[1:]),
            out_specs=[whole(o) for o in outs] + here(apart),
            scratch_shapes=[
                pltpu.VMEM((4, T, D), bf16),
                pltpu.VMEM((W // C, C, D), bf16),
                dma((13,)),
                dma((W // C,)),
            ],
        ),
    )
    r2, r1, r3 = to_x(p2, 2), to_x(p1, 1), to_x(p3, 3)
    pre_b = to_core(pre_other.reshape(T, FF))
    r3, inputs = barrier((r3, inputs))
    got = [to_l(inputs, k) for k in (1, 2, 3)]
    r1, r2, r3, pre_b, *got = barrier((r1, r2, r3, pre_b, *got))

    (sent,) = call(sum_kernel, "back_sum", [message(T)], (own, r1, r2, r3, top_y))
    other = to_h(sent)
    pre, sent, *got = barrier((pre.reshape(2, T, FF), sent, *got))
    pre_far = to_x(pre, 2)
    outs = [like(T, D), like(8, 128, dtype=f32)]
    token_inputs, _ = call(stack_kernel, "stack_inputs", outs, (inputs, *got))
    token_inputs = ring(token_inputs, to_y)
    outs = [like(4, T, D)]
    (inputs_all,) = call(
        join_kernel, "join_inputs", outs, token_inputs, in_specs=here(token_inputs), out_specs=here(outs), scratch_shapes=[dma((4,))]
    )
    other, pre_far, inputs_all = barrier((other, pre_far, inputs_all))
    pre_a = pre[0]
    (msg,) = call(slope_kernel, "slope", [message(T)], (sent, other, pre_a, pre_b))
    msgs = ring(msg, to_x)
    stacked, _ = barrier((stacked.reshape(4 * T, D), msg))
    stacked_o = to_core(stacked)
    inputs_all, _ = barrier((inputs_all, msg))
    inputs_o = to_core(inputs_all)
    *far, stacked_o, inputs_o = barrier((*msgs[1:], stacked_o, inputs_o))
    msgs = [msgs[0], *far]

    args = (at, *msgs, w_in, w_in_o)
    outs = [like(T, D, dtype=f32)] + [message(T)] * 3
    apart = [like(4 * T, FF)] * 2
    own, p1, p2, p3, hq_a, hq_b = call(
        grad_kernel,
        "input_grad",
        outs + apart,
        args,
        big,
        20,
        grid_spec=pltpu.PrefetchScalarGridSpec(
            num_scalar_prefetch=1,
            grid=(D // C,),
            in_specs=here(args[1:]),
            out_specs=[whole(o) for o in outs] + here(apart),
            scratch_shapes=[
                pltpu.VMEM((4, *message(T).shape), bf16),
                pltpu.VMEM((2, D // C, C, FF), bf16),
                dma((52,)),
                dma((2, D // C)),
            ],
        ),
    )
    r2, r1, r3 = to_y(p2, 2), to_y(p1, 1), to_y(p3, 3)
    pre, hq_b = barrier((pre, hq_b))
    pre_near, pre_behind = to_x(pre, 3), to_x(pre, 1)
    args = (pre, pre_near, pre_far, pre_behind, stacked, stacked_o)
    (w_out_grad,) = call(
        w_out_kernel,
        "w_out_grad",
        [like(FF, D)],
        args,
        big,
        20,
        grid=(steps,),
        in_specs=here(args),
        out_specs=[pl.BlockSpec((FF, B), lambda i: (0, i))],
        scratch_shapes=[
            pltpu.VMEM((4, 2, T, FF), bf16),
            pltpu.VMEM((2, 4 * T, FF), bf16),
            pltpu.VMEM((steps, 2, 4 * T, B), bf16),
            dma((4,)),
            dma((2, steps)),
        ],
    )
    r1, r2, r3, w_out_grad, hq_b = barrier((r1, r2, r3, w_out_grad, hq_b))
    outs = [like(32, D, dtype=f32)] + [message(32)] * 3
    kept, s1, s2, s3 = call(gather_kernel, "y_sum", outs, (own, r1, r2, r3, p1))
    r2, r3, r1 = to_l(s2, 2), to_l(s3, 3), to_l(s1, 1)
    hq_o = to_core(hq_b)
    args = (at, inputs_all, inputs_o, hq_a, hq_o)
    (w_in_grad,) = call(
        w_in_kernel,
        "w_in_grad",
        [like(D, FF)],
        args,
        big,
        20,
        grid_spec=pltpu.PrefetchScalarGridSpec(
            num_scalar_prefetch=1,
            grid=(steps,),
            in_specs=here(args[1:]),
            out_specs=[pl.BlockSpec((B, FF), lambda i, t: (i, 0))],
            scratch_shapes=[
                pltpu.VMEM((2, 4, T, FF), bf16),
                pltpu.VMEM((steps, 2, 4, T, B), bf16),
                dma((8,)),
                dma((2, steps)),
            ],
        ),
    )
    r1, r2, r3, w_in_grad = barrier((r1, r2, r3, w_in_grad))
    outs = [like(32, D), like(8, 128, dtype=f32)]
    input_grad, tops = call(last_kernel, "l_sum", outs, (kept, r1, r2, r3, s1))
    amaxes = jnp.max(jnp.maximum(tops, to_core(tops)), axis=1)[:2]
    return (input_grad, w_in_grad, w_out_grad, amaxes)


def solution(mesh):
    placed = (P("col", "row"), P("row", "col"), P("row", "col"), P("col", "row"), P("col", "row"))
    return jax.shard_map(
        local,
        mesh=mesh,
        in_specs=placed,
        out_specs=(P("col", "row"), P("row", "col"), P("col", "row"), P()),
        check_vma=False,
    )
```

```python
import math

import jax
import jax.numpy as jnp
from jax import lax
from jax.experimental import pallas as pl
from jax.experimental.pallas import tpu as pltpu
from jax.sharding import PartitionSpec as P

coef = math.sqrt(2.0 / math.pi)
f32, bf16 = jnp.float32, jnp.bfloat16
barrier = lax.optimization_barrier
D, FF, T = 1536, 768, 128
W = 2 * FF
B, C = 512, 768


def gelu_value(pre):
    inner = coef * (pre + 0.044715 * pre * pre * pre)
    return 0.5 * pre * (1.0 + jnp.tanh(inner))


def gelu_slope(pre):
    inner = coef * (pre + 0.044715 * pre * pre * pre)
    tval = jnp.tanh(inner)
    return 0.5 * (1.0 + tval) + 0.5 * pre * (1.0 - tval * tval) * coef * (
        1.0 + 3.0 * 0.044715 * pre * pre
    )


def across(left, right):
    return lax.dot_general(left, right, (((1,), (1,)), ((), ())), preferred_element_type=f32)


def over_tokens(left, right):
    return lax.dot_general(left, right, (((0,), (0,)), ((), ())), preferred_element_type=f32)


def to_core(v):
    return lax.ppermute(v, "col", [(i, i ^ 1) for i in range(32)])


def to_l(v, k):
    return lax.ppermute(v, "col", [(i, i ^ (2 * k)) for i in range(32)])


def to_y(v, k):
    return lax.ppermute(v, "col", [(i, (i + 8 * k) % 32) for i in range(32)])


def to_x(v, k):
    return lax.ppermute(v, "row", [(i, (i + 2 * k) % 8) for i in range(8)])


def to_h(v):
    return lax.ppermute(v, "row", [(i, i ^ 1) for i in range(8)])


def ring(v, send):
    far, near, behind = send(v, 2), send(v, 3), send(v, 1)
    return [v, near, far, behind]


def message(rows):
    return like(W // 128 * rows + 16, 128)


def tile(c, rows, first=0, count=None):
    return slice(c * rows + first, c * rows + first + (count or rows))


def put_tops(ref, top_h, top_y):
    row = lax.broadcasted_iota(jnp.int32, (16, 128), 0)
    high = top_h.astype(bf16).astype(f32)
    mid = (top_h - high).astype(bf16).astype(f32)
    low = top_h - high - mid
    extra = jnp.where(row == 0, high, jnp.where(row == 1, mid, jnp.where(row == 2, low, 0.0)))
    ref[ref.shape[0] - 16 :] = jnp.where(row == 3, top_y, extra).astype(bf16)


def get_tops(refs):
    top_h = top_y = jnp.zeros((1, 128), f32)
    for ref in refs:
        extra = ref[ref.shape[0] - 16 :].astype(f32)
        top_h = jnp.maximum(top_h, extra[0:1] + extra[1:2] + extra[2:3])
        top_y = jnp.maximum(top_y, extra[3:4])
    return top_h, top_y


def columns(c):
    return slice(c * 128, (c + 1) * 128)


def stack_kernel(a0, a1, a2, a3, stacked, tops):
    for m, a in enumerate((a0, a1, a2, a3)):
        stacked[m * 32 : (m + 1) * 32] = a[...]
    top = jnp.max(jnp.abs(a0[...].astype(f32)), axis=0, keepdims=True)
    lanes = top[:, :128]
    for k in range(1, D // 128):
        lanes = jnp.maximum(lanes, top[:, 128 * k : 128 * (k + 1)])
    tops[...] = jnp.broadcast_to(lanes, (8, 128))


def join_kernel(a0, a1, a2, a3, out, sems):
    moves = [copy(a, out.at[k], sems.at[k]) for k, a in enumerate((a0, a1, a2, a3))]
    for move in moves:
        move.start()
    for move in moves:
        move.wait()


def place(at):
    row, col = at[0], at[1]
    return row >> 1, row & 1, col >> 3, (col >> 1) & 3, col & 1


def copy(src, dst, sem):
    return pltpu.make_async_copy(src, dst, sem)


def back_kernel(
    t, g0, g1, g2, g3, wa, wb, here, there, own, p1, p2, p3, stacked, pre, pre_other, blocks, weights, sems, wsems
):
    i = pl.program_id(0)
    x, h, y, l, c = place(t)
    shift = x - y
    last = FF // C

    def weight(k):
        ref, at = (wa, k) if k < last else (wb, k - last)
        return copy(ref.at[at * C : (at + 1) * C], weights.at[k], wsems.at[k])

    def moves():
        out = []
        for high in range(2):
            for low in range(2):
                for core in range(2):
                    rows = slice((low * 2 + core) * 32, (low * 2 + core + 1) * 32)
                    ref, slot = (here, there)[high], (2 * (h ^ high) + low) ^ l
                    out.append(copy(ref.at[rows], pre.at[c ^ core, slot], sems.at[5 + len(out)]))
        return out

    def blocks_in():
        return [copy(g, blocks.at[(s - shift) & 3], sems.at[s]) for s, g in enumerate((g0, g1, g2, g3))]

    @pl.when(i == 0)
    def _():
        for move in blocks_in():
            move.start()
        for k in range(W // C):
            weight(k).start()
        for move in moves():
            move.start()
        for move in blocks_in():
            move.wait()
        copy(blocks, stacked, sems.at[4]).start()

    for k in range(W // C):
        pl.when(i == k)(weight(k).wait)
    out = across(blocks[...].reshape(4 * T, D), weights[i])
    at = pl.ds(pl.multiple_of(i * C, C), C)
    own[:, at] = out[:T]
    for k, p in enumerate((p1, p2, p3)):
        p[:, at] = out[(k + 1) * T : (k + 2) * T].astype(bf16)

    @pl.when(i == 0)
    def _():
        for move in moves():
            move.wait()
        copy(pre.at[1], pre_other, sems.at[5]).start()

    @pl.when(i == pl.num_programs(0) - 1)
    def _():
        copy(pre.at[1], pre_other, sems.at[5]).wait()
        copy(blocks, stacked, sems.at[4]).wait()


def sum_kernel(own, r1, r2, r3, tops, msg):
    for c in range(W // 128):
        at = (slice(None), columns(c))
        total = own[at] + r1[at].astype(f32) + r2[at].astype(f32) + r3[at].astype(f32)
        msg[tile(c, T)] = total.astype(bf16)
    put_tops(msg, jnp.zeros((1, 128), f32), tops[0:1])


def slope_kernel(mine, other, pre_a, pre_b, msg):
    _, top_y = get_tops((mine, other))
    top_h = jnp.zeros((1, 128), f32)
    for c in range(W // 128):
        pre, k = (pre_a, c) if c < FF // 128 else (pre_b, c - FF // 128)
        back = mine[tile(c, T)].astype(f32) + other[tile(c, T)].astype(f32)
        hidden_grad = back * gelu_slope(pre[:, columns(k)].astype(f32))
        top_h = jnp.maximum(top_h, jnp.max(jnp.abs(hidden_grad), axis=0, keepdims=True))
        msg[tile(c, T)] = hidden_grad.astype(bf16)
    put_tops(msg, top_h, top_y)


def grad_kernel(t, m0, m1, m2, m3, wa, wb, own, p1, p2, p3, hq_a, hq_b, blocks, weights, sems, wsems):
    i = pl.program_id(0)
    x, _, y, _, _ = place(t)
    half = FF // 128

    def weight(k):
        rows = slice(k * C, (k + 1) * C)
        return [copy(w.at[rows], weights.at[s, k], wsems.at[s, k]) for s, w in enumerate((wa, wb))]

    def blocks_in():
        return [copy(m, blocks.at[(s - y + x) & 3], sems.at[s]) for s, m in enumerate((m0, m1, m2, m3))]

    def blocks_out():
        return [
            copy(
                blocks.at[(s - y + x) & 3, tile(k * half + c, T)],
                out.at[s * T : (s + 1) * T, columns(c)],
                sems.at[4 + (k * 4 + s) * half + c],
            )
            for k, out in enumerate((hq_a, hq_b))
            for s in range(4)
            for c in range(half)
        ]

    @pl.when(i == 0)
    def _():
        for move in blocks_in():
            move.start()
        for k in range(D // C):
            for move in weight(k):
                move.start()
        for move in blocks_in():
            move.wait()
        for move in blocks_out():
            move.start()
        top_h, top_y = get_tops([blocks.at[s] for s in range(4)])
        for p in (p1, p2, p3):
            put_tops(p, top_h, top_y)

    for k in range(D // C):

        @pl.when(i == k)
        def _():
            for move in weight(k):
                move.wait()

    tiles = [blocks[:, tile(c, T)].reshape(4 * T, 128) for c in range(2 * half)]
    hq = [jnp.concatenate(part, axis=1) for part in (tiles[:half], tiles[half:])]
    out = across(hq[0], weights[0, i]) + across(hq[1], weights[1, i])
    own[:, pl.ds(pl.multiple_of(i * C, C), C)] = out[:T]
    for k, p in enumerate((p1, p2, p3)):
        for c in range(C // 128):
            rows = pl.ds(pl.multiple_of((i * (C // 128) + c) * T, T), T)
            p[rows] = out[(k + 1) * T : (k + 2) * T, columns(c)].astype(bf16)

    @pl.when(i == pl.num_programs(0) - 1)
    def _():
        for move in blocks_out():
            move.wait()


def gather_kernel(own, r1, r2, r3, mine, kept, s1, s2, s3):
    top_h, top_y = get_tops((r1, r2, r3, mine))
    for m, out in enumerate((kept, s1, s2, s3)):
        for c in range(D // 128):
            at = tile(c, T, 32 * m, 32)
            total = own[32 * m : 32 * (m + 1), columns(c)]
            total = total + r1[at].astype(f32) + r2[at].astype(f32) + r3[at].astype(f32)
            if m:
                out[tile(c, 32)] = total.astype(bf16)
            else:
                out[:, columns(c)] = total
    for out in (s1, s2, s3):
        put_tops(out, top_h, top_y)


def last_kernel(kept, r1, r2, r3, mine, out, tops):
    top_h, top_y = get_tops((r1, r2, r3, mine))
    for c in range(D // 128):
        at = tile(c, 32)
        total = kept[:, columns(c)] + r1[at].astype(f32) + r2[at].astype(f32) + r3[at].astype(f32)
        out[:, columns(c)] = total.astype(bf16)
    row = lax.broadcasted_iota(jnp.int32, (8, 128), 0)
    tops[...] = jnp.where(row == 0, top_y, jnp.where(row == 1, top_h, 0.0))


def w_out_kernel(r0, r1, r2, r3, mine, other, out, raw, hidden, grads, sems, gsems):
    i = pl.program_id(0)

    def parts(k):
        cols = slice(k * B, (k + 1) * B)
        return [copy(g.at[:, cols], grads.at[k, s], gsems.at[s, k]) for s, g in enumerate((mine, other))]

    def pres():
        return [copy(r, raw.at[s], sems.at[s]) for s, r in enumerate((r0, r1, r2, r3))]

    @pl.when(i == 0)
    def _():
        for move in pres():
            move.start()
        for k in range(D // B):
            for move in parts(k):
                move.start()
        for s, move in enumerate(pres()):
            move.wait()
            for c in range(2):
                hidden[c, s * T : (s + 1) * T] = gelu_value(raw[s, c].astype(f32)).astype(bf16)

    for k in range(D // B):

        @pl.when(i == k)
        def _():
            for move in parts(k):
                move.wait()

    half = grads[i]
    out[...] = (over_tokens(hidden[0], half[0]) + over_tokens(hidden[1], half[1])).astype(bf16)


def w_in_kernel(t, inputs, inputs_o, mine, other, out, hq, cols, sems, csems):
    i = pl.program_id(0)
    x, _, y, _, _ = place(t)

    def parts(k):
        at = slice(k * B, (k + 1) * B)
        return [copy(a.at[:, :, at], cols.at[k, s], csems.at[s, k]) for s, a in enumerate((inputs, inputs_o))]

    def blocks_in():
        return [
            copy(ref.at[k * T : (k + 1) * T], hq.at[s, (k + x - y) & 3], sems.at[4 * s + k])
            for s, ref in enumerate((mine, other))
            for k in range(4)
        ]

    @pl.when(i == 0)
    def _():
        for move in blocks_in():
            move.start()
        for k in range(D // B):
            for move in parts(k):
                move.start()
        for move in blocks_in():
            move.wait()

    for k in range(D // B):

        @pl.when(i == k)
        def _():
            for move in parts(k):
                move.wait()

    out[...] = over_tokens(cols[i].reshape(8 * T, B), hq[...].reshape(8 * T, FF)).astype(bf16)


def like(*shape, dtype=bf16):
    return jax.ShapeDtypeStruct(shape, dtype)


def call(kernel, name, outs, args, flops=0, mib=8, light=False, **spec):
    outs = list(outs)
    size = sum(math.prod(a.shape) * a.dtype.itemsize for a in list(args) + outs)
    return pl.pallas_call(
        kernel,
        out_shape=outs,
        name=name,
        compiler_params=pltpu.CompilerParams(vmem_limit_bytes=mib * 2**20),
        cost_estimate=pl.CostEstimate(flops=flops, bytes_accessed=1 if light else size, transcendentals=0),
        **spec,
    )(*args)


def whole(a):
    zeros = (0,) * len(a.shape)
    return pl.BlockSpec(a.shape, lambda i, *t: zeros, pipeline_mode=pl.Buffered(1))


def here(args):
    return [pl.BlockSpec(memory_space=pltpu.HBM)] * len(args)


dma = pltpu.SemaphoreType.DMA


def local(inputs, preact, w_in, w_out, out_grad):
    row, col = lax.axis_index("row"), lax.axis_index("col")
    at, out_grad, inputs = barrier((jnp.stack([row, col]).astype(jnp.int32), out_grad, inputs))
    steps = D // B
    big = 2 * 4 * T * D * W

    got = [to_l(out_grad, k) for k in (1, 2, 3)]
    w_out_o = to_core(w_out)
    *got, w_out_o, pre_late, w_in_late = barrier((*got, w_out_o, preact, w_in))
    outs = [like(T, D), like(8, 128, dtype=f32)]
    grad, top_y = call(stack_kernel, "stack", outs, (out_grad, *got))
    grads = ring(grad, to_y)
    w_in_o = to_core(w_in_late)
    there = to_h(pre_late)
    *grads, w_in_o, there = barrier((*grads, w_in_o, there))

    args = (at, *grads, w_out, w_out_o, preact, there)
    outs = [like(T, W, dtype=f32)] + [like(T, W)] * 3
    apart = [like(4, T, D), like(2, 4, 32, FF), like(4, 32, FF)]
    own, p1, p2, p3, stacked, pre, pre_other = call(
        back_kernel,
        "back",
        outs + apart,
        args,
        big,
        20,
        grid_spec=pltpu.PrefetchScalarGridSpec(
            num_scalar_prefetch=1,
            grid=(W // C,),
            in_specs=here(args[1:]),
            out_specs=[whole(o) for o in outs] + here(apart),
            scratch_shapes=[
                pltpu.VMEM((4, T, D), bf16),
                pltpu.VMEM((W // C, C, D), bf16),
                dma((13,)),
                dma((W // C,)),
            ],
        ),
    )
    r2, r1, r3 = to_x(p2, 2), to_x(p1, 1), to_x(p3, 3)
    pre_b = to_core(pre_other.reshape(T, FF))
    r3, inputs = barrier((r3, inputs))
    got = [to_l(inputs, k) for k in (1, 2, 3)]
    r1, r2, r3, pre_b, *got = barrier((r1, r2, r3, pre_b, *got))

    (sent,) = call(sum_kernel, "back_sum", [message(T)], (own, r1, r2, r3, top_y))
    other = to_h(sent)
    pre, sent, *got = barrier((pre.reshape(2, T, FF), sent, *got))
    pre_far = to_x(pre, 2)
    outs = [like(T, D), like(8, 128, dtype=f32)]
    token_inputs, _ = call(stack_kernel, "stack_inputs", outs, (inputs, *got))
    token_inputs = ring(token_inputs, to_y)
    outs = [like(4, T, D)]
    (inputs_all,) = call(
        join_kernel, "join_inputs", outs, token_inputs, in_specs=here(token_inputs), out_specs=here(outs), scratch_shapes=[dma((4,))]
    )
    other, pre_far, inputs_all = barrier((other, pre_far, inputs_all))
    pre_a = pre[0]
    (msg,) = call(slope_kernel, "slope", [message(T)], (sent, other, pre_a, pre_b))
    msgs = ring(msg, to_x)
    stacked, _ = barrier((stacked.reshape(4 * T, D), msg))
    stacked_o = to_core(stacked)
    inputs_all, _ = barrier((inputs_all, msg))
    inputs_o = to_core(inputs_all)
    *far, stacked_o, inputs_o = barrier((*msgs[1:], stacked_o, inputs_o))
    msgs = [msgs[0], *far]

    args = (at, *msgs, w_in, w_in_o)
    outs = [like(T, D, dtype=f32)] + [message(T)] * 3
    apart = [like(4 * T, FF)] * 2
    own, p1, p2, p3, hq_a, hq_b = call(
        grad_kernel,
        "input_grad",
        outs + apart,
        args,
        big,
        20,
        grid_spec=pltpu.PrefetchScalarGridSpec(
            num_scalar_prefetch=1,
            grid=(D // C,),
            in_specs=here(args[1:]),
            out_specs=[whole(o) for o in outs] + here(apart),
            scratch_shapes=[
                pltpu.VMEM((4, *message(T).shape), bf16),
                pltpu.VMEM((2, D // C, C, FF), bf16),
                dma((52,)),
                dma((2, D // C)),
            ],
        ),
    )
    r2, r1, r3 = to_y(p2, 2), to_y(p1, 1), to_y(p3, 3)
    pre, hq_b = barrier((pre, hq_b))
    pre_near, pre_behind = to_x(pre, 3), to_x(pre, 1)
    args = (pre, pre_near, pre_far, pre_behind, stacked, stacked_o)
    (w_out_grad,) = call(
        w_out_kernel,
        "w_out_grad",
        [like(FF, D)],
        args,
        1,
        20,
        True,
        grid=(steps,),
        in_specs=here(args),
        out_specs=[pl.BlockSpec((FF, B), lambda i: (0, i))],
        scratch_shapes=[
            pltpu.VMEM((4, 2, T, FF), bf16),
            pltpu.VMEM((2, 4 * T, FF), bf16),
            pltpu.VMEM((steps, 2, 4 * T, B), bf16),
            dma((4,)),
            dma((2, steps)),
        ],
    )
    r1, r2, r3, w_out_grad, hq_b = barrier((r1, r2, r3, w_out_grad, hq_b))
    outs = [like(32, D, dtype=f32)] + [message(32)] * 3
    kept, s1, s2, s3 = call(gather_kernel, "y_sum", outs, (own, r1, r2, r3, p1))
    r2, r3, r1 = to_l(s2, 2), to_l(s3, 3), to_l(s1, 1)
    hq_o = to_core(hq_b)
    args = (at, inputs_all, inputs_o, hq_a, hq_o)
    (w_in_grad,) = call(
        w_in_kernel,
        "w_in_grad",
        [like(D, FF)],
        args,
        big,
        20,
        grid_spec=pltpu.PrefetchScalarGridSpec(
            num_scalar_prefetch=1,
            grid=(steps,),
            in_specs=here(args[1:]),
            out_specs=[pl.BlockSpec((B, FF), lambda i, t: (i, 0))],
            scratch_shapes=[
                pltpu.VMEM((2, 4, T, FF), bf16),
                pltpu.VMEM((steps, 2, 4, T, B), bf16),
                dma((8,)),
                dma((2, steps)),
            ],
        ),
    )
    r1, r2, r3, w_in_grad = barrier((r1, r2, r3, w_in_grad))
    outs = [like(32, D), like(8, 128, dtype=f32)]
    input_grad, tops = call(last_kernel, "l_sum", outs, (kept, r1, r2, r3, s1))
    amaxes = jnp.max(jnp.maximum(tops, to_core(tops)), axis=1)[:2]
    return (input_grad, w_in_grad, w_out_grad, amaxes)


def solution(mesh):
    placed = (P("col", "row"), P("row", "col"), P("row", "col"), P("col", "row"), P("col", "row"))
    return jax.shard_map(
        local,
        mesh=mesh,
        in_specs=placed,
        out_specs=(P("col", "row"), P("row", "col"), P("col", "row"), P()),
        check_vma=False,
    )
```

```python
import math

import jax
import jax.numpy as jnp
from jax import lax
from jax.experimental import pallas as pl
from jax.experimental.pallas import tpu as pltpu
from jax.sharding import PartitionSpec as P

coef = math.sqrt(2.0 / math.pi)
f32, bf16 = jnp.float32, jnp.bfloat16
barrier = lax.optimization_barrier
D, FF, T = 1536, 768, 128
W = 2 * FF
B, C = 768, 768


def gelu_value(pre):
    inner = coef * (pre + 0.044715 * pre * pre * pre)
    return 0.5 * pre * (1.0 + jnp.tanh(inner))


def gelu_slope(pre):
    inner = coef * (pre + 0.044715 * pre * pre * pre)
    tval = jnp.tanh(inner)
    return 0.5 * (1.0 + tval) + 0.5 * pre * (1.0 - tval * tval) * coef * (
        1.0 + 3.0 * 0.044715 * pre * pre
    )


def across(left, right):
    return lax.dot_general(left, right, (((1,), (1,)), ((), ())), preferred_element_type=f32)


def over_tokens(left, right):
    return lax.dot_general(left, right, (((0,), (0,)), ((), ())), preferred_element_type=f32)


def to_core(v):
    return lax.ppermute(v, "col", [(i, i ^ 1) for i in range(32)])


def to_l(v, k):
    return lax.ppermute(v, "col", [(i, i ^ (2 * k)) for i in range(32)])


def to_y(v, k):
    return lax.ppermute(v, "col", [(i, (i + 8 * k) % 32) for i in range(32)])


def to_x(v, k):
    return lax.ppermute(v, "row", [(i, (i + 2 * k) % 8) for i in range(8)])


def to_h(v):
    return lax.ppermute(v, "row", [(i, i ^ 1) for i in range(8)])


def ring(v, send):
    far, near, behind = send(v, 2), send(v, 3), send(v, 1)
    return [v, near, far, behind]


def message(rows):
    return like(W // 128 * rows + 16, 128)


def tile(c, rows, first=0, count=None):
    return slice(c * rows + first, c * rows + first + (count or rows))


def put_tops(ref, top_h, top_y):
    row = lax.broadcasted_iota(jnp.int32, (16, 128), 0)
    high = top_h.astype(bf16).astype(f32)
    mid = (top_h - high).astype(bf16).astype(f32)
    low = top_h - high - mid
    extra = jnp.where(row == 0, high, jnp.where(row == 1, mid, jnp.where(row == 2, low, 0.0)))
    ref[ref.shape[0] - 16 :] = jnp.where(row == 3, top_y, extra).astype(bf16)


def get_tops(refs):
    top_h = top_y = jnp.zeros((1, 128), f32)
    for ref in refs:
        extra = ref[ref.shape[0] - 16 :].astype(f32)
        top_h = jnp.maximum(top_h, extra[0:1] + extra[1:2] + extra[2:3])
        top_y = jnp.maximum(top_y, extra[3:4])
    return top_h, top_y


def columns(c):
    return slice(c * 128, (c + 1) * 128)


def first_kernel(a, stacked, tops):
    stacked[:32] = a[...]
    top = jnp.max(jnp.abs(a[...].astype(f32)), axis=0, keepdims=True)
    lanes = top[:, :128]
    for k in range(1, D // 128):
        lanes = jnp.maximum(lanes, top[:, 128 * k : 128 * (k + 1)])
    tops[...] = jnp.broadcast_to(lanes, (8, 128))


def stack_kernel(so_far, a1, a2, a3, stacked):
    stacked[:32] = so_far[:32]
    for m, a in enumerate((a1, a2, a3)):
        stacked[(m + 1) * 32 : (m + 2) * 32] = a[...]


def join_kernel(a0, a1, a2, a3, out, sems):
    moves = [copy(a, out.at[k], sems.at[k]) for k, a in enumerate((a0, a1, a2, a3))]
    for move in moves:
        move.start()
    for move in moves:
        move.wait()


def place(at):
    row, col = at[0], at[1]
    return row >> 1, row & 1, col >> 3, (col >> 1) & 3, col & 1


def copy(src, dst, sem):
    return pltpu.make_async_copy(src, dst, sem)


def back_kernel(
    t, g0, g1, g2, g3, wa, wb, here, there, own, p1, p2, p3, stacked, pre, pre_other, blocks, weights, sems, wsems
):
    i = pl.program_id(0)
    x, h, y, l, c = place(t)
    shift = x - y
    last = FF // C

    def weight(k):
        ref, at = (wa, k) if k < last else (wb, k - last)
        return copy(ref.at[at * C : (at + 1) * C], weights.at[k], wsems.at[k])

    def moves():
        out = []
        for high in range(2):
            for low in range(2):
                for core in range(2):
                    rows = slice((low * 2 + core) * 32, (low * 2 + core + 1) * 32)
                    ref, slot = (here, there)[high], (2 * (h ^ high) + low) ^ l
                    out.append(copy(ref.at[rows], pre.at[c ^ core, slot], sems.at[5 + len(out)]))
        return out

    def blocks_in():
        return [copy(g, blocks.at[(s - shift) & 3], sems.at[s]) for s, g in enumerate((g0, g1, g2, g3))]

    @pl.when(i == 0)
    def _():
        for move in blocks_in():
            move.start()
        for k in range(W // C):
            weight(k).start()
        for move in moves():
            move.start()
        for move in blocks_in():
            move.wait()
        copy(blocks, stacked, sems.at[4]).start()

    for k in range(W // C):
        pl.when(i == k)(weight(k).wait)
    out = across(blocks[...].reshape(4 * T, D), weights[i])
    at = pl.ds(pl.multiple_of(i * C, C), C)
    own[:, at] = out[:T]
    for k, p in enumerate((p1, p2, p3)):
        p[:, at] = out[(k + 1) * T : (k + 2) * T].astype(bf16)

    @pl.when(i == 0)
    def _():
        for move in moves():
            move.wait()
        copy(pre.at[1], pre_other, sems.at[5]).start()

    @pl.when(i == pl.num_programs(0) - 1)
    def _():
        copy(pre.at[1], pre_other, sems.at[5]).wait()
        copy(blocks, stacked, sems.at[4]).wait()


def sum_kernel(own, r1, r2, r3, tops, msg):
    for c in range(W // 128):
        at = (slice(None), columns(c))
        total = own[at] + r1[at].astype(f32) + r2[at].astype(f32) + r3[at].astype(f32)
        msg[tile(c, T)] = total.astype(bf16)
    put_tops(msg, jnp.zeros((1, 128), f32), tops[0:1])


def slope_kernel(mine, other, pre_a, pre_b, msg):
    _, top_y = get_tops((mine, other))
    top_h = jnp.zeros((1, 128), f32)
    for c in range(W // 128):
        pre, k = (pre_a, c) if c < FF // 128 else (pre_b, c - FF // 128)
        back = mine[tile(c, T)].astype(f32) + other[tile(c, T)].astype(f32)
        hidden_grad = back * gelu_slope(pre[:, columns(k)].astype(f32))
        top_h = jnp.maximum(top_h, jnp.max(jnp.abs(hidden_grad), axis=0, keepdims=True))
        msg[tile(c, T)] = hidden_grad.astype(bf16)
    put_tops(msg, top_h, top_y)


def grad_kernel(t, m0, m1, m2, m3, wa, wb, own, p1, p2, p3, hq_a, hq_b, blocks, weights, sems, wsems):
    i = pl.program_id(0)
    x, _, y, _, _ = place(t)
    half = FF // 128

    def weight(k):
        rows = slice(k * C, (k + 1) * C)
        return [copy(w.at[rows], weights.at[s, k], wsems.at[s, k]) for s, w in enumerate((wa, wb))]

    def blocks_in():
        return [copy(m, blocks.at[(s - y + x) & 3], sems.at[s]) for s, m in enumerate((m0, m1, m2, m3))]

    def blocks_out():
        return [
            copy(
                blocks.at[(s - y + x) & 3, tile(k * half + c, T)],
                out.at[s * T : (s + 1) * T, columns(c)],
                sems.at[4 + (k * 4 + s) * half + c],
            )
            for k, out in enumerate((hq_a, hq_b))
            for s in range(4)
            for c in range(half)
        ]

    @pl.when(i == 0)
    def _():
        for move in blocks_in():
            move.start()
        for k in range(D // C):
            for move in weight(k):
                move.start()
        for move in blocks_in():
            move.wait()
        for move in blocks_out():
            move.start()
        top_h, top_y = get_tops([blocks.at[s] for s in range(4)])
        for p in (p1, p2, p3):
            put_tops(p, top_h, top_y)

    for k in range(D // C):

        @pl.when(i == k)
        def _():
            for move in weight(k):
                move.wait()

    tiles = [blocks[:, tile(c, T)].reshape(4 * T, 128) for c in range(2 * half)]
    hq = [jnp.concatenate(part, axis=1) for part in (tiles[:half], tiles[half:])]
    out = across(hq[0], weights[0, i]) + across(hq[1], weights[1, i])
    own[:, pl.ds(pl.multiple_of(i * C, C), C)] = out[:T]
    for k, p in enumerate((p1, p2, p3)):
        for c in range(C // 128):
            rows = pl.ds(pl.multiple_of((i * (C // 128) + c) * T, T), T)
            p[rows] = out[(k + 1) * T : (k + 2) * T, columns(c)].astype(bf16)

    @pl.when(i == pl.num_programs(0) - 1)
    def _():
        for move in blocks_out():
            move.wait()


def gather_kernel(own, r1, r2, r3, mine, kept, s1, s2, s3):
    top_h, top_y = get_tops((r1, r2, r3, mine))
    for m, out in enumerate((kept, s1, s2, s3)):
        for c in range(D // 128):
            at = tile(c, T, 32 * m, 32)
            total = own[32 * m : 32 * (m + 1), columns(c)]
            total = total + r1[at].astype(f32) + r2[at].astype(f32) + r3[at].astype(f32)
            if m:
                out[tile(c, 32)] = total.astype(bf16)
            else:
                out[:, columns(c)] = total
    for out in (s1, s2, s3):
        put_tops(out, top_h, top_y)


def last_kernel(kept, r1, r2, r3, mine, out, tops):
    top_h, top_y = get_tops((r1, r2, r3, mine))
    for c in range(D // 128):
        at = tile(c, 32)
        total = kept[:, columns(c)] + r1[at].astype(f32) + r2[at].astype(f32) + r3[at].astype(f32)
        out[:, columns(c)] = total.astype(bf16)
    row = lax.broadcasted_iota(jnp.int32, (8, 128), 0)
    tops[...] = jnp.where(row == 0, top_y, jnp.where(row == 1, top_h, 0.0))


def w_out_kernel(r0, r1, r2, r3, mine, other, out, raw, hidden, grads, sems, gsems):
    i = pl.program_id(0)

    def parts(k):
        cols = slice(k * B, (k + 1) * B)
        return [copy(g.at[:, cols], grads.at[k, s], gsems.at[s, k]) for s, g in enumerate((mine, other))]

    def pres():
        return [copy(r, raw.at[s], sems.at[s]) for s, r in enumerate((r0, r1, r2, r3))]

    @pl.when(i == 0)
    def _():
        for move in pres():
            move.start()
        for k in range(D // B):
            for move in parts(k):
                move.start()
        for s, move in enumerate(pres()):
            move.wait()
            for c in range(2):
                hidden[c, s * T : (s + 1) * T] = gelu_value(raw[s, c].astype(f32)).astype(bf16)

    for k in range(D // B):

        @pl.when(i == k)
        def _():
            for move in parts(k):
                move.wait()

    half = grads[i]
    out[...] = (over_tokens(hidden[0], half[0]) + over_tokens(hidden[1], half[1])).astype(bf16)


def w_in_kernel(t, inputs, inputs_o, mine, other, out, hq, cols, sems, csems):
    i = pl.program_id(0)
    x, _, y, _, _ = place(t)

    def parts(k):
        at = slice(k * B, (k + 1) * B)
        return [copy(a.at[:, :, at], cols.at[k, s], csems.at[s, k]) for s, a in enumerate((inputs, inputs_o))]

    def blocks_in():
        return [
            copy(ref.at[k * T : (k + 1) * T], hq.at[s, (k + x - y) & 3], sems.at[4 * s + k])
            for s, ref in enumerate((mine, other))
            for k in range(4)
        ]

    @pl.when(i == 0)
    def _():
        for move in blocks_in():
            move.start()
        for k in range(D // B):
            for move in parts(k):
                move.start()
        for move in blocks_in():
            move.wait()

    for k in range(D // B):

        @pl.when(i == k)
        def _():
            for move in parts(k):
                move.wait()

    out[...] = over_tokens(cols[i].reshape(8 * T, B), hq[...].reshape(8 * T, FF)).astype(bf16)


def like(*shape, dtype=bf16):
    return jax.ShapeDtypeStruct(shape, dtype)


def call(kernel, name, outs, args, flops=0, mib=8, light=False, **spec):
    outs = list(outs)
    size = sum(math.prod(a.shape) * a.dtype.itemsize for a in list(args) + outs)
    return pl.pallas_call(
        kernel,
        out_shape=outs,
        name=name,
        compiler_params=pltpu.CompilerParams(vmem_limit_bytes=mib * 2**20),
        cost_estimate=pl.CostEstimate(flops=flops, bytes_accessed=1 if light else size, transcendentals=0),
        **spec,
    )(*args)


def whole(a):
    zeros = (0,) * len(a.shape)
    return pl.BlockSpec(a.shape, lambda i, *t: zeros, pipeline_mode=pl.Buffered(1))


def here(args):
    return [pl.BlockSpec(memory_space=pltpu.HBM)] * len(args)


dma = pltpu.SemaphoreType.DMA


def local(inputs, preact, w_in, w_out, out_grad):
    row, col = lax.axis_index("row"), lax.axis_index("col")
    at, out_grad, inputs = barrier((jnp.stack([row, col]).astype(jnp.int32), out_grad, inputs))
    steps = D // B
    big = 2 * 4 * T * D * W

    got = [to_l(out_grad, k) for k in (1, 2, 3)]
    w_out_o = to_core(w_out)
    outs = [like(T, D), like(8, 128, dtype=f32)]
    grad, top_y = call(first_kernel, "first", outs, (out_grad,))
    *got, grad, top_y, w_out_o, pre_late, w_in_late = barrier((*got, grad, top_y, w_out_o, preact, w_in))
    (grad,) = call(stack_kernel, "stack", outs[:1], (grad, *got), input_output_aliases={0: 0})
    grads = ring(grad, to_y)
    w_in_o = to_core(w_in_late)
    there = to_h(pre_late)
    *grads, w_in_o, there = barrier((*grads, w_in_o, there))

    args = (at, *grads, w_out, w_out_o, preact, there)
    outs = [like(T, W, dtype=f32)] + [like(T, W)] * 3
    apart = [like(4, T, D), like(2, 4, 32, FF), like(4, 32, FF)]
    own, p1, p2, p3, stacked, pre, pre_other = call(
        back_kernel,
        "back",
        outs + apart,
        args,
        big,
        20,
        grid_spec=pltpu.PrefetchScalarGridSpec(
            num_scalar_prefetch=1,
            grid=(W // C,),
            in_specs=here(args[1:]),
            out_specs=[whole(o) for o in outs] + here(apart),
            scratch_shapes=[
                pltpu.VMEM((4, T, D), bf16),
                pltpu.VMEM((W // C, C, D), bf16),
                dma((13,)),
                dma((W // C,)),
            ],
        ),
    )
    r2, r1, r3 = to_x(p2, 2), to_x(p1, 1), to_x(p3, 3)
    pre_b = to_core(pre_other.reshape(T, FF))
    r3, inputs = barrier((r3, inputs))
    got = [to_l(inputs, k) for k in (1, 2, 3)]
    outs = [like(T, D), like(8, 128, dtype=f32)]
    token_inputs, _ = call(first_kernel, "first_inputs", outs, (inputs,))
    r1, r2, r3, pre_b, token_inputs, *got = barrier((r1, r2, r3, pre_b, token_inputs, *got))

    (sent,) = call(sum_kernel, "back_sum", [message(T)], (own, r1, r2, r3, top_y))
    other = to_h(sent)
    pre, sent, *got = barrier((pre.reshape(2, T, FF), sent, *got))
    pre_far = to_x(pre, 2)
    (token_inputs,) = call(stack_kernel, "stack_inputs", [like(T, D)], (token_inputs, *got), input_output_aliases={0: 0})
    token_inputs = ring(token_inputs, to_y)
    outs = [like(4, T, D)]
    (inputs_all,) = call(
        join_kernel, "join_inputs", outs, token_inputs, in_specs=here(token_inputs), out_specs=here(outs), scratch_shapes=[dma((4,))]
    )
    other, pre_far, inputs_all = barrier((other, pre_far, inputs_all))
    pre_a = pre[0]
    (msg,) = call(slope_kernel, "slope", [message(T)], (sent, other, pre_a, pre_b))
    msgs = ring(msg, to_x)
    stacked, _ = barrier((stacked.reshape(4 * T, D), msg))
    stacked_o = to_core(stacked)
    inputs_all, _ = barrier((inputs_all, msg))
    inputs_o = to_core(inputs_all)
    *far, stacked_o, inputs_o = barrier((*msgs[1:], stacked_o, inputs_o))
    msgs = [msgs[0], *far]

    args = (at, *msgs, w_in, w_in_o)
    outs = [like(T, D, dtype=f32)] + [message(T)] * 3
    apart = [like(4 * T, FF)] * 2
    own, p1, p2, p3, hq_a, hq_b = call(
        grad_kernel,
        "input_grad",
        outs + apart,
        args,
        big,
        20,
        grid_spec=pltpu.PrefetchScalarGridSpec(
            num_scalar_prefetch=1,
            grid=(D // C,),
            in_specs=here(args[1:]),
            out_specs=[whole(o) for o in outs] + here(apart),
            scratch_shapes=[
                pltpu.VMEM((4, *message(T).shape), bf16),
                pltpu.VMEM((2, D // C, C, FF), bf16),
                dma((52,)),
                dma((2, D // C)),
            ],
        ),
    )
    r2, r1, r3 = to_y(p2, 2), to_y(p1, 1), to_y(p3, 3)
    pre, hq_b = barrier((pre, hq_b))
    pre_near, pre_behind = to_x(pre, 3), to_x(pre, 1)
    args = (pre, pre_near, pre_far, pre_behind, stacked, stacked_o)
    (w_out_grad,) = call(
        w_out_kernel,
        "w_out_grad",
        [like(FF, D)],
        args,
        1,
        20,
        True,
        grid=(steps,),
        in_specs=here(args),
        out_specs=[pl.BlockSpec((FF, B), lambda i: (0, i))],
        scratch_shapes=[
            pltpu.VMEM((4, 2, T, FF), bf16),
            pltpu.VMEM((2, 4 * T, FF), bf16),
            pltpu.VMEM((steps, 2, 4 * T, B), bf16),
            dma((4,)),
            dma((2, steps)),
        ],
    )
    r1, r2, r3, w_out_grad, hq_b = barrier((r1, r2, r3, w_out_grad, hq_b))
    outs = [like(32, D, dtype=f32)] + [message(32)] * 3
    kept, s1, s2, s3 = call(gather_kernel, "y_sum", outs, (own, r1, r2, r3, p1))
    r2, r3, r1 = to_l(s2, 2), to_l(s3, 3), to_l(s1, 1)
    hq_o = to_core(hq_b)
    args = (at, inputs_all, inputs_o, hq_a, hq_o)
    (w_in_grad,) = call(
        w_in_kernel,
        "w_in_grad",
        [like(D, FF)],
        args,
        big,
        20,
        grid_spec=pltpu.PrefetchScalarGridSpec(
            num_scalar_prefetch=1,
            grid=(steps,),
            in_specs=here(args[1:]),
            out_specs=[pl.BlockSpec((B, FF), lambda i, t: (i, 0))],
            scratch_shapes=[
                pltpu.VMEM((2, 4, T, FF), bf16),
                pltpu.VMEM((steps, 2, 4, T, B), bf16),
                dma((8,)),
                dma((2, steps)),
            ],
        ),
    )
    r1, r2, r3, w_in_grad = barrier((r1, r2, r3, w_in_grad))
    outs = [like(32, D), like(8, 128, dtype=f32)]
    input_grad, tops = call(last_kernel, "l_sum", outs, (kept, r1, r2, r3, s1))
    amaxes = jnp.max(jnp.maximum(tops, to_core(tops)), axis=1)[:2]
    return (input_grad, w_in_grad, w_out_grad, amaxes)


def solution(mesh):
    placed = (P("col", "row"), P("row", "col"), P("row", "col"), P("col", "row"), P("col", "row"))
    return jax.shard_map(
        local,
        mesh=mesh,
        in_specs=placed,
        out_specs=(P("col", "row"), P("row", "col"), P("col", "row"), P()),
        check_vma=False,
    )
```
